256 devices in a mesh: sx: 8 (over z), sy: 16 (over y, x), dp: 2 (over core).
Axes of the slice: x: 4, y: 4, z: 8, core: 2. Of those that a mesh axis runs over, the one named last changes fastest.
Arguments:
- features: bfloat16 [2, 64, 128, 4, 8, 128], P('dp', 'sx', 'sy'), may hold values from -6 to 6
- cotangent: bfloat16 [2, 64, 128, 4, 8, 128], P('dp', 'sx', 'sy'), may hold values from -6 to 6
- first_weight: bfloat16 [27, 128, 128], replicated, may hold values from -0.109375 to 0.109375
- second_weight: bfloat16 [27, 128, 128], replicated, may hold values from -0.109375 to 0.109375
- neighbours: int32 [2, 8, 16, 4, 26], P('dp', 'sx', 'sy'), may hold values from -1 to 3, as said below
- counts: int32 [2, 8, 16], P('dp', 'sx', 'sy'), may hold values from 1 to 4, as said below
Outputs:
- out_field: bfloat16 [2, 64, 128, 4, 8, 128], P('dp', 'sx', 'sy')
- grad_input: bfloat16 [2, 64, 128, 4, 8, 128], P('dp', 'sx', 'sy')
- grad_first: float32 [27, 128, 128], replicated
- grad_second: float32 [27, 128, 128], replicated
The draws below stay inside these ranges and needn't reach their ends.
Inputs may be any that keep to these rules, and one draw needn't show every extreme that they name: Entries name only live slots; slots at or above a column's count have no neighbours; the relation is symmetric: if slot s of column (i, j) names slot t in direction d, then slot t of column (i+dx, j+dy) names s in the opposite direction, and the blocks are adjacent in space; columns outside the grid are never named. `counts`: some column of every workpiece has 4 live slots.
All inputs are finite; a program needn't handle non-finite values.
Results may differ from the reference program's by a relative error of at most 0.012.
Values may be sent and summed in bfloat16 or wider, within the bound.
No kernel may reach another device: no remote copies, remote signals or barrier semaphores. Data moves between devices by JAX's collectives and lax.ppermute only.
A program may use at most 192 MiB of HBM per device.

```python
import jax
import jax.numpy as jnp
from jax import lax

C = 128
BE = 8
NB = 4
BATCH = 2
COLS_X = 8
COLS_Y = 16
XV = 64
YV = 128


def column_layout(key):
    height_key = jax.random.fold_in(key, 7)
    count_key = jax.random.fold_in(key, 11)
    chosen_key = jax.random.fold_in(key, 13)
    heights = jax.random.randint(height_key, (BATCH, COLS_X, COLS_Y), 0, 2)
    drawn = jax.random.randint(count_key, (BATCH, COLS_X * COLS_Y), 1, NB + 1)
    chosen = jax.random.randint(chosen_key, (BATCH,), 0, COLS_X * COLS_Y)
    forced = jnp.arange(COLS_X * COLS_Y)[None, :] == chosen[:, None]
    counts = jnp.where(forced, NB, drawn).reshape(BATCH, COLS_X, COLS_Y)
    return (heights.astype(jnp.int32), counts.astype(jnp.int32))


def draw_counts(key, part):
    heights, counts = column_layout(key)
    return counts


def draw_neighbours(key, part):
    heights, counts = column_layout(key)
    slot_ids = jnp.arange(NB, dtype=jnp.int32)
    height_pad = jnp.pad(heights, ((0, 0), (1, 1), (1, 1)))
    count_pad = jnp.pad(counts, ((0, 0), (1, 1), (1, 1)))
    entries = []
    for shift_x in range(3):
        for shift_y in range(3):
            for shift_z in range(3):
                if shift_x * 9 + shift_y * 3 + shift_z == 13:
                    continue
                near_height = height_pad[:, shift_x:shift_x + COLS_X, shift_y:shift_y + COLS_Y]
                near_count = count_pad[:, shift_x:shift_x + COLS_X, shift_y:shift_y + COLS_Y]
                target = heights[..., None] + slot_ids + (shift_z - 1) - near_height[..., None]
                valid = (target >= 0) & (target < near_count[..., None]) & (slot_ids < counts[..., None])
                entries.append(jnp.where(valid, target, -1))
    return jnp.stack(entries, axis=-1).astype(jnp.int32)


def shard_levels(rng, extent, cuts, least, top_value):
    def one(axis_at, parts):
        steps = jax.random.uniform(jax.random.fold_in(jax.random.fold_in(rng, 6), axis_at), (parts,), jnp.float32, least / len(cuts), top_value / len(cuts))
        return jnp.repeat(jnp.exp(steps), extent[axis_at] // parts).reshape((-1,) + (1,) * (len(extent) - axis_at - 1))

    level = one(*cuts[0])
    for cut in cuts[1:]:
        level = level * one(*cut)
    return level


def normal_values(key, shape, scale, limit, split=(), kind=jnp.bfloat16):
    gain = shard_levels(key, shape, split, -0.22, 0.18) if split else 1.0
    values = jax.random.normal(key, shape, jnp.float32) * scale * gain
    return jnp.minimum(jnp.maximum(values, -limit), limit).astype(kind)


def setup_inputs(seed: int = 0) -> dict:
    streams_of = jax.random.split(jax.random.key(seed), 7)
    return {
        "features": normal_values(streams_of[0], (BATCH, XV, YV, NB, BE, C), 1.0, 6.0, ((0, 2), (1, 8), (2, 16))),
        "cotangent": normal_values(streams_of[1], (BATCH, XV, YV, NB, BE, C), 1.0, 6.0, ((0, 2), (1, 8), (2, 16))),
        "first_weight": normal_values(streams_of[2], (27, C, C), (27 * C) ** -0.5, 0.109375),
        "second_weight": normal_values(streams_of[3], (27, C, C), (27 * C) ** -0.5, 0.109375),
        "neighbours": draw_neighbours(jax.random.fold_in(streams_of[6], 71), 0),
        "counts": draw_counts(jax.random.fold_in(streams_of[6], 71), 0),
    }


def padded_blocks(halo_field, neighbour):
    block_edge = halo_field.shape[0] - 2
    ranges_xy = [(0, 1), (1, block_edge + 1), (block_edge + 1, block_edge + 2)]
    ranges_z = [(block_edge - 1, block_edge), (0, block_edge), (0, 1)]
    planes = []
    for shift_x in range(3):
        row_list = []
        for shift_y in range(3):
            slab_list = []
            for shift_z in range(3):
                direction = shift_x * 9 + shift_y * 3 + shift_z
                low_x, high_x = ranges_xy[shift_x]
                low_y, high_y = ranges_xy[shift_y]
                low_z, high_z = ranges_z[shift_z]
                region = halo_field[low_x:high_x, low_y:high_y, :, low_z:high_z]
                if direction == 13:
                    slab_piece = region
                else:
                    entry = direction if direction < 13 else direction - 1
                    target = neighbour[:, entry]
                    valid = (target >= 0).astype(region.dtype)[None, None, :, None, None]
                    slab_piece = jnp.take(region, jnp.maximum(target, 0), axis=2) * valid
                slab_list.append(slab_piece)
            row_list.append(jnp.concatenate(slab_list, axis=3))
        planes.append(jnp.concatenate(row_list, axis=1))
    return jnp.concatenate(planes, axis=0)


def patch_matrix(padded, block_edge):
    pieces = []
    for shift_x in range(3):
        for shift_y in range(3):
            for shift_z in range(3):
                pieces.append(padded[shift_x:shift_x + block_edge, shift_y:shift_y + block_edge, :, shift_z:shift_z + block_edge])
    stacked = jnp.concatenate(pieces, axis=-1)
    return stacked.reshape(-1, stacked.shape[-1])


def flipped_weight(weight):
    return jnp.transpose(weight[::-1], (0, 2, 1))


def silu_slope(values):
    logistic = jax.nn.sigmoid(values)
    return logistic * (1.0 + values * (1.0 - logistic))


def column_start(column_x, column_y):
    zero_index = jnp.zeros((), jnp.int32)
    start_x = (column_x * BE).astype(jnp.int32)
    start_y = (column_y * BE).astype(jnp.int32)
    return (start_x, start_y, zero_index, zero_index, zero_index)


def column_patches(padded_field, neighbours_w, column_id):
    column_x = (column_id // COLS_Y).astype(jnp.int32)
    column_y = (column_id % COLS_Y).astype(jnp.int32)
    halo_field = lax.dynamic_slice(padded_field, column_start(column_x, column_y), (BE + 2, BE + 2, NB, BE, C))
    return patch_matrix(padded_blocks(halo_field, neighbours_w[column_x, column_y]), BE)


def pad_field(field):
    return jnp.pad(field, ((1, 1), (1, 1), (0, 0), (0, 0), (0, 0)))


def convolve_field(field, neighbours_w, weight):
    padded_field = pad_field(field)
    matrix = weight.reshape(27 * C, C)

    def per_column(column_id):
        columns = column_patches(padded_field, neighbours_w, column_id)
        return jnp.dot(columns, matrix, preferred_element_type=jnp.float32).reshape(BE, BE, NB, BE, C)

    result = lax.map(per_column, jnp.arange(COLS_X * COLS_Y, dtype=jnp.int32))
    result = result.reshape(COLS_X, COLS_Y, BE, BE, NB, BE, C)
    return jnp.transpose(result, (0, 2, 1, 3, 4, 5, 6)).reshape(XV, YV, NB, BE, C)


def weight_grad_field(field, grad_field, neighbours_w):
    padded_field = pad_field(field)

    def advance(running, column_id):
        columns = column_patches(padded_field, neighbours_w, column_id)
        column_x = (column_id // COLS_Y).astype(jnp.int32)
        column_y = (column_id % COLS_Y).astype(jnp.int32)
        grads = lax.dynamic_slice(grad_field, column_start(column_x, column_y), (BE, BE, NB, BE, C)).reshape(-1, C)
        term = lax.dot_general(columns, grads, (((0,), (0,)), ((), ())), preferred_element_type=jnp.float32)
        return running + term, None

    running, unused = lax.scan(advance, jnp.zeros((27 * C, C), jnp.float32), jnp.arange(COLS_X * COLS_Y, dtype=jnp.int32))
    return running.reshape(27, C, C)


def live_field(counts_w):
    live_mask = (jnp.arange(NB, dtype=jnp.int32)[None, None, :] < counts_w[:, :, None]).astype(jnp.float32)
    live_mask = jnp.repeat(jnp.repeat(live_mask, BE, axis=0), BE, axis=1)
    return live_mask[:, :, :, None, None]


def reference(features, cotangent, first_weight, second_weight, neighbours, counts):
    grad_scale = float(BATCH * COLS_X * COLS_Y * NB * BE ** 3) ** -0.5
    flip_first = flipped_weight(first_weight)
    flip_second = flipped_weight(second_weight)
    outputs = []
    input_grads = []
    first_total = jnp.zeros((27, C, C), jnp.float32)
    second_total = jnp.zeros((27, C, C), jnp.float32)
    for member in range(BATCH):
        live_mask = live_field(counts[member])
        links = neighbours[member]
        masked = features[member] * live_mask.astype(features.dtype)
        pre_first = convolve_field(masked, links, first_weight)
        hidden = (jax.nn.silu(pre_first) * live_mask).astype(jnp.bfloat16)
        pre_second = convolve_field(hidden, links, second_weight)
        summed = masked.astype(jnp.float32) + pre_second
        outputs.append((jax.nn.silu(summed) * live_mask).astype(jnp.bfloat16))
        back_second = (cotangent[member].astype(jnp.float32) * silu_slope(summed) * live_mask).astype(jnp.bfloat16)
        second_total = second_total + weight_grad_field(hidden, back_second, links)
        back_hidden = convolve_field(back_second, links, flip_second)
        back_first = (back_hidden * silu_slope(pre_first) * live_mask).astype(jnp.bfloat16)
        first_total = first_total + weight_grad_field(masked, back_first, links)
        back_input = convolve_field(back_first, links, flip_first)
        input_grads.append(((back_second.astype(jnp.float32) + back_input) * live_mask).astype(jnp.bfloat16))
    return (jnp.stack(outputs), jnp.stack(input_grads), first_total * grad_scale, second_total * grad_scale)
```

```python
import functools

import jax
import jax.numpy as jnp
from jax import lax
from jax.experimental import pallas as pl
from jax.experimental.pallas import tpu as pltpu
from jax.sharding import PartitionSpec as P

C = 128
BE = 8
NB = 4
ROWS = NB * BE
ZERO = ROWS
F32 = jnp.float32
BF16 = jnp.bfloat16
COLUMNS = [(cx, cy) for cx in (-1, 0, 1) for cy in (-1, 0, 1)]
OWN = 4


def shift_pair(low, high, axis):
    ends = lax.axis_size(axis) - 1
    from_low = lax.ppermute(high, axis, [(i, i + 1) for i in range(ends)])
    from_high = lax.ppermute(low, axis, [(i + 1, i) for i in range(ends)])
    return from_low, from_high


def spans(halo):
    return {-1: (0, halo), 0: (halo, halo + BE), 1: (halo + BE, 2 * halo + BE)}


def build_patches(tab, field, put, halo, column, xs, ys):
    cx, cy = COLUMNS[column]
    row = lax.broadcasted_iota(jnp.int32, (1, BE, C), 1)
    for sx, (x0, x1) in spans(halo).items():
        xa, xb = max(x0, xs[0]), min(x1, xs[1] + 2)
        if xa >= xb:
            continue
        for sy, (y0, y1) in spans(halo).items():
            ya, yb = max(y0, ys[0]), min(y1, ys[1] + 2)
            if ya >= yb:
                continue
            first = (sx - cx + 1) * 9 + (sy - cy + 1) * 3
            offsets = [
                [pl.multiple_of(tab[column * C + s * 27 + first + j], BE) for j in range(3)]
                for s in range(NB)
            ]

            def line(x):
                parts = [[], [], []]
                for below, here, above in offsets:
                    v = field[x, ya:yb, pl.ds(here, BE), :]
                    lo = field[x, ya:yb, pl.ds(below, BE), :]
                    hi = field[x, ya:yb, pl.ds(above, BE), :]
                    parts[0].append(pltpu.roll(jnp.where(row == BE - 1, lo, v), 1, 1))
                    parts[1].append(v)
                    parts[2].append(pltpu.roll(jnp.where(row == 0, hi, v), BE - 1, 1))
                for j in range(3):
                    value = jnp.concatenate(parts[j], axis=1).astype(BF16)
                    put(x - xs[0], ya - ys[0], yb - ys[0], j * C, value)

            if xb - xa > 3:

                def body(x, unused):
                    line(x)
                    return unused

                lax.fori_loop(xa, xb, body, 0)
            else:
                for x in range(xa, xb):
                    line(x)


def into(ref, lead=None):
    def put(x, ya, yb, lane, value):
        if lead is None:
            ref[x, ya:yb, :, lane : lane + C] = value
        else:
            ref[lead, x, ya:yb, :, lane : lane + C] = value

    return put


def product(get, weight):
    parts = []
    for a in range(3):
        for b in range(3):
            piece = get(a, b)
            parts.append(piece.reshape(-1, piece.shape[-1]))
    return jnp.dot(jnp.concatenate(parts, axis=1), weight[...], preferred_element_type=F32)


def rounded(value):
    return value.astype(BF16).astype(F32)


def slope_of(value):
    sig = jax.nn.sigmoid(value)
    return sig * (1.0 + value * (1.0 - sig))


def live_rows(tab):
    parts = [
        jnp.where(tab[OWN * C + s * 27 + 13] < ZERO, jnp.ones((BE, C), F32), jnp.zeros((BE, C), F32))
        for s in range(NB)
    ]
    return jnp.concatenate(parts, axis=0)


def zero_slot(field):
    def body(x, unused):
        field[x, :, ZERO : ZERO + BE, :] = jnp.zeros((field.shape[1], BE, C), F32)
        return unused

    lax.fori_loop(0, field.shape[0], body, 0)


def rows_at(field, x, y, value):
    n, m = value.shape[:2]
    field[x : x + n, y : y + m, 0:ROWS, :] = value


def weight_grad(patch, grads, turned, out, base, scale):
    for x in range(BE):
        block = grads[x].reshape(BE * ROWS, C).astype(F32)
        turned[:, x * BE * ROWS : (x + 1) * BE * ROWS] = block.T.astype(BF16)

    def body(i, unused):
        a, b = i // 3, i % 3
        right = patch[pl.ds(a, BE), pl.ds(b, BE)].reshape(BE * BE * ROWS, 3 * C)
        term = jnp.dot(turned[...], right, preferred_element_type=F32) * scale
        for j in range(3):
            at = pl.multiple_of(base + (i * 3 + j) * C, C)
            out[pl.ds(at, C), :] = term[:, j * C : (j + 1) * C].T.astype(BF16)
        return unused

    lax.fori_loop(0, 9, body, 0)


def main_kernel(scale, tab, x, cot, xm, xp, ym, yp, w1, w2, w2f, out, b2o, b1o, gr,
                field, hid, back, p1, p2, px, py, pc, slope1, turned):
    live = live_rows(tab)
    for ref in (field, hid, back):
        zero_slot(ref)

    def fill(i, unused):
        field[3 + i, 3:11, 0:ROWS, :] = x[i].astype(F32)
        return unused

    lax.fori_loop(0, BE, fill, 0)
    for i in range(3):
        rows_at(field, i, 3, xm[8 * i : 8 * i + 8].astype(F32)[None])
        rows_at(field, 11 + i, 3, xp[8 * i : 8 * i + 8].astype(F32)[None])

    def fill_sides(i, unused):
        field[i, 0:3, 0:ROWS, :] = ym[pl.ds(3 * i, 3)].astype(F32)
        field[i, 11:14, 0:ROWS, :] = yp[pl.ds(3 * i, 3)].astype(F32)
        return unused

    lax.fori_loop(0, 14, fill_sides, 0)

    ends = spans(2)
    corners = [0, 2, 6, 8]
    build_patches(tab, field, into(p1), 3, OWN, ends[0], ends[0])
    for j, cx in enumerate((-1, 1)):
        build_patches(tab, field, into(px, j), 3, COLUMNS.index((cx, 0)), ends[cx], ends[0])
        build_patches(tab, field, into(py, j), 3, COLUMNS.index((0, cx)), ends[0], ends[cx])
    for j, c in enumerate(corners):
        build_patches(tab, field, into(pc, j), 3, c, ends[COLUMNS[c][0]], ends[COLUMNS[c][1]])

    def first_own(i, unused):
        pre = product(lambda a, b: p1[pl.ds(2 * i + a, 2), b : b + BE], w1)
        slope1[pl.ds(2 * i, 2)] = slope_of(pre).reshape(2, BE, ROWS, C)
        hid[pl.ds(2 + 2 * i, 2), 2:10, 0:ROWS, :] = rounded(pre * jax.nn.sigmoid(pre)).reshape(2, BE, ROWS, C)
        return unused

    lax.fori_loop(0, 4, first_own, 0)
    for j, at in enumerate((0, 10)):
        pre = product(lambda a, b: px[j, a : a + 2, b : b + BE], w1)
        rows_at(hid, at, 2, rounded(pre * jax.nn.sigmoid(pre)).reshape(2, BE, ROWS, C))
        pre = product(lambda a, b: py[j, a : a + BE, b : b + 2], w1)
        rows_at(hid, 2, at, rounded(pre * jax.nn.sigmoid(pre)).reshape(BE, 2, ROWS, C))
    pre = product(lambda a, b: pc[:, a : a + 2, b : b + 2], w1)
    value = rounded(pre * jax.nn.sigmoid(pre)).reshape(4, 2, 2, ROWS, C)
    for j, (ax, ay) in enumerate(((0, 0), (0, 10), (10, 0), (10, 10))):
        rows_at(hid, ax, ay, value[j])

    ends = spans(1)
    build_patches(tab, hid, into(p2), 2, OWN, ends[0], ends[0])
    for j, cx in enumerate((-1, 1)):
        build_patches(tab, hid, into(px, j), 2, COLUMNS.index((cx, 0)), ends[cx], ends[0])
        build_patches(tab, hid, into(py, j), 2, COLUMNS.index((0, cx)), ends[0], ends[cx])
    for j, c in enumerate(corners):
        build_patches(tab, hid, into(pc, j), 2, c, ends[COLUMNS[c][0]], ends[COLUMNS[c][1]])

    def second_own(i, unused):
        pre = product(lambda a, b: p2[pl.ds(2 * i + a, 2), b : b + BE], w2).reshape(2, BE, ROWS, C)
        total = field[pl.ds(3 + 2 * i, 2), 3:11, 0:ROWS, :] * live + pre
        sig = jax.nn.sigmoid(total)
        out[pl.ds(2 * i, 2)] = (total * sig * live).astype(BF16)
        slope = sig * (1.0 + total * (1.0 - sig))
        grad = (cot[pl.ds(2 * i, 2)].astype(F32) * slope * live).astype(BF16)
        b2o[pl.ds(2 * i, 2)] = grad
        back[pl.ds(1 + 2 * i, 2), 1:9, 0:ROWS, :] = grad.astype(F32)
        return unused

    lax.fori_loop(0, 4, second_own, 0)
    pre = product(lambda a, b: px[:, a : a + 1, b : b + BE], w2).reshape(2, BE, ROWS, C)
    for j, (at, cx, near) in enumerate(((2, 0, xm), (11, 9, xp))):
        total = field[at, 3:11, 0:ROWS, :] + pre[j]
        grad = near[24:32].astype(F32) * slope_of(total)
        rows_at(back, cx, 1, rounded(grad)[None])
    pre = product(lambda a, b: py[:, a : a + BE, b : b + 1], w2).reshape(2, BE, ROWS, C)
    for j, (at, cy, near) in enumerate(((2, 0, ym), (11, 9, yp))):
        total = field[3:11, at, 0:ROWS, :] + pre[j]
        grad = near[43:51].astype(F32) * slope_of(total)
        back[1:9, cy, 0:ROWS, :] = rounded(grad)
    pre = product(lambda a, b: pc[:, a : a + 1, b : b + 1], w2).reshape(4, ROWS, C)
    for j, (ax, ay, cx, cy, near, at) in enumerate(
        ((2, 2, 0, 0, ym, 42), (2, 11, 0, 9, yp, 42), (11, 2, 9, 0, ym, 51), (11, 11, 9, 9, yp, 51))
    ):
        total = field[ax, ay, 0:ROWS, :] + pre[j]
        grad = near[at].astype(F32) * slope_of(total)
        back[cx, cy, 0:ROWS, :] = rounded(grad)
    weight_grad(p2, b2o, turned, gr, 27 * C, scale)

    build_patches(tab, back, into(p2), 1, OWN, (0, BE), (0, BE))

    def third(i, unused):
        pre = product(lambda a, b: p2[pl.ds(2 * i + a, 2), b : b + BE], w2f).reshape(2, BE, ROWS, C)
        b1o[pl.ds(2 * i, 2)] = (pre * slope1[pl.ds(2 * i, 2)] * live).astype(BF16)
        return unused

    lax.fori_loop(0, 4, third, 0)
    weight_grad(p1, b1o, turned, gr, 0, scale)


def last_kernel(tab, b1, b2, xm, xp, ym, yp, w1f, out, field, patch):
    live = live_rows(tab)
    zero_slot(field)

    def fill(i, unused):
        field[1 + i, 1:9, 0:ROWS, :] = b1[i].astype(F32)
        return unused

    lax.fori_loop(0, BE, fill, 0)
    rows_at(field, 0, 1, xm[...].astype(F32)[None])
    rows_at(field, 9, 1, xp[...].astype(F32)[None])
    field[:, 0, 0:ROWS, :] = ym[...].astype(F32)
    field[:, 9, 0:ROWS, :] = yp[...].astype(F32)
    build_patches(tab, field, into(patch), 1, OWN, (0, BE), (0, BE))

    def step(i, unused):
        pre = product(lambda a, b: patch[pl.ds(2 * i + a, 2), b : b + BE], w1f).reshape(2, BE, ROWS, C)
        out[pl.ds(2 * i, 2)] = ((b2[pl.ds(2 * i, 2)].astype(F32) + pre) * live).astype(BF16)
        return unused

    lax.fori_loop(0, 4, step, 0)


def call(kernel, outs, scratch, cost, *args):
    smem = pl.BlockSpec(memory_space=pltpu.SMEM)
    vmem = pl.BlockSpec(memory_space=pltpu.VMEM)
    return pl.pallas_call(
        kernel,
        out_shape=outs,
        in_specs=[smem] + [vmem] * (len(args) - 1),
        out_specs=jax.tree.map(lambda o: vmem, outs),
        scratch_shapes=scratch,
        compiler_params=pltpu.CompilerParams(vmem_limit_bytes=48 * 2**20),
        cost_estimate=cost,
    )(*args)


def reduce_axis(part, axis):
    n = lax.axis_size(axis)
    swapped = lax.all_to_all(part.reshape(n, part.shape[0] // n, C), axis, 0, 0, tiled=True)
    return jnp.sum(swapped.astype(F32), axis=0).astype(BF16)


def gather_axis(part, axis):
    n = lax.axis_size(axis)
    copies = jnp.broadcast_to(part[None], (n,) + part.shape)
    return lax.all_to_all(copies, axis, 0, 0, tiled=True).reshape(n * part.shape[0], C)


def flipped_weight(weight):
    return jnp.transpose(weight[::-1], (0, 2, 1)).reshape(27 * C, C)


def shards(features, cotangent, first_weight, second_weight, neighbours, counts):
    x = features.reshape(BE, BE, ROWS, C)
    cot = cotangent.reshape(BE, BE, ROWS, C)
    n_devices = lax.axis_size("sx") * lax.axis_size("sy") * lax.axis_size("dp")
    scale = float(n_devices * NB * BE**3) ** -0.5

    links = neighbours.reshape(NB, 26)
    slots = jnp.arange(NB, dtype=jnp.int32)
    centre = jnp.where(slots < counts.reshape(()), slots, -1)[:, None]
    named = jnp.concatenate([links[:, :13], centre, links[:, 13:]], axis=1)
    starts = jnp.where(named < 0, NB, named) * BE
    table = jnp.pad(starts.reshape(NB * 27), (0, C - NB * 27))
    tline = jnp.broadcast_to(table.astype(BF16)[None, None], (1, ROWS, C))

    def lines(value):
        return value.reshape(-1, ROWS, C)

    low = jnp.concatenate([lines(x[0:3]), cot[0], tline], axis=0)
    high = jnp.concatenate([lines(x[5:8]), cot[7], tline], axis=0)
    xm, xp = shift_pair(low, high, "sx")
    xmf, xpf = (v[:24].reshape(3, BE, ROWS, C) for v in (xm, xp))

    def side(ys, y):
        return jnp.concatenate(
            [lines(xmf[:, ys]), lines(x[:, ys]), lines(xpf[:, ys]), xm[24 + y : 25 + y], cot[:, y], xp[24 + y : 25 + y],
             xm[32:33], tline, xp[32:33]],
            axis=0,
        )

    ym, yp = shift_pair(side(slice(0, 3), 0), side(slice(5, 8), 7), "sy")
    tabs = jnp.stack(
        [ym[52, 0], xm[32, 0], yp[52, 0], ym[53, 0], tline[0, 0], yp[53, 0], ym[54, 0], xp[32, 0], yp[54, 0]]
    ).astype(jnp.int32).reshape(9 * C)

    block = jax.ShapeDtypeStruct((BE, BE, ROWS, C), BF16)
    lanes = 3 * C
    unit = 2 * BE * BE * ROWS * 27 * C * C
    out, b2, b1, grads = call(
        functools.partial(main_kernel, scale),
        [block, block, block, jax.ShapeDtypeStruct((54 * C, C), BF16)],
        [
            pltpu.VMEM((14, 14, ROWS + BE, C), F32),
            pltpu.VMEM((12, 12, ROWS + BE, C), F32),
            pltpu.VMEM((10, 10, ROWS + BE, C), F32),
            pltpu.VMEM((10, 10, ROWS, lanes), BF16),
            pltpu.VMEM((10, 10, ROWS, lanes), BF16),
            pltpu.VMEM((2, 4, 10, ROWS, lanes), BF16),
            pltpu.VMEM((2, 10, 4, ROWS, lanes), BF16),
            pltpu.VMEM((4, 4, 4, ROWS, lanes), BF16),
            pltpu.VMEM((BE, BE, ROWS, C), F32),
            pltpu.VMEM((C, BE * BE * ROWS), BF16),
        ],
        pl.CostEstimate(flops=7 * unit, bytes_accessed=10 * 2**20, transcendentals=2**20),
        tabs, x, cot, xm, xp, ym, yp,
        first_weight.reshape(27 * C, C), second_weight.reshape(27 * C, C), flipped_weight(second_weight),
    )

    bxm, bxp = shift_pair(b1[0], b1[7], "sx")
    bym, byp = shift_pair(
        jnp.concatenate([bxm[0:1], b1[:, 0], bxp[0:1]], axis=0),
        jnp.concatenate([bxm[7:8], b1[:, 7], bxp[7:8]], axis=0),
        "sy",
    )
    grad_input = call(
        last_kernel,
        block,
        [pltpu.VMEM((10, 10, ROWS + BE, C), F32), pltpu.VMEM((10, 10, ROWS, lanes), BF16)],
        pl.CostEstimate(flops=unit, bytes_accessed=4 * 2**20, transcendentals=0),
        tabs, b1, b2, bxm, bxp, bym, byp, flipped_weight(first_weight),
    )

    for axis in ("dp", "sy", "sx"):
        grads = reduce_axis(grads, axis)
    for axis in ("sx", "sy", "dp"):
        grads = gather_axis(grads, axis)
    grads = grads.reshape(2, 27, C, C).astype(F32)
    shape = features.shape
    return out.reshape(shape), grad_input.reshape(shape), grads[0], grads[1]


def solution(mesh):
    column = P("dp", "sx", "sy", None, None, None)
    return jax.shard_map(
        shards,
        mesh=mesh,
        in_specs=(column, column, P(), P(), P("dp", "sx", "sy", None, None), P("dp", "sx", "sy")),
        out_specs=(column, column, P(), P()),
        check_vma=False,
    )
```

```python
import functools

import jax
import jax.numpy as jnp
from jax import lax
from jax.experimental import pallas as pl
from jax.experimental.pallas import tpu as pltpu
from jax.sharding import PartitionSpec as P

C = 128
BE = 8
NB = 4
ROWS = NB * BE
ZERO = ROWS
F32 = jnp.float32
BF16 = jnp.bfloat16
COLUMNS = [(cx, cy) for cx in (-1, 0, 1) for cy in (-1, 0, 1)]
OWN = 4


def shift_pair(low, high, axis):
    ends = lax.axis_size(axis) - 1
    from_low = lax.ppermute(high, axis, [(i, i + 1) for i in range(ends)])
    from_high = lax.ppermute(low, axis, [(i + 1, i) for i in range(ends)])
    return from_low, from_high


def spans(halo):
    return {-1: (0, halo), 0: (halo, halo + BE), 1: (halo + BE, 2 * halo + BE)}


def build_patches(tab, field, put, halo, column, xs, ys):
    cx, cy = COLUMNS[column]
    row = lax.broadcasted_iota(jnp.int32, (1, BE, C), 1)
    for sx, (x0, x1) in spans(halo).items():
        xa, xb = max(x0, xs[0]), min(x1, xs[1] + 2)
        if xa >= xb:
            continue
        for sy, (y0, y1) in spans(halo).items():
            ya, yb = max(y0, ys[0]), min(y1, ys[1] + 2)
            if ya >= yb:
                continue
            first = (sx - cx + 1) * 9 + (sy - cy + 1) * 3
            offsets = [
                [pl.multiple_of(tab[column, s * 27 + first + j], BE) for j in range(3)]
                for s in range(NB)
            ]

            def line(x):
                parts = [[], [], []]
                for below, here, above in offsets:
                    v = field[x, ya:yb, pl.ds(here, BE), :]
                    lo = field[x, ya:yb, pl.ds(below, BE), :]
                    hi = field[x, ya:yb, pl.ds(above, BE), :]
                    parts[0].append(pltpu.roll(jnp.where(row == BE - 1, lo, v), 1, 1))
                    parts[1].append(v)
                    parts[2].append(pltpu.roll(jnp.where(row == 0, hi, v), BE - 1, 1))
                for j in range(3):
                    value = jnp.concatenate(parts[j], axis=1).astype(BF16)
                    put(x - xs[0], ya - ys[0], yb - ys[0], j * C, value)

            if xb - xa > 3:

                def body(x, unused):
                    line(x)
                    return unused

                lax.fori_loop(xa, xb, body, 0)
            else:
                for x in range(xa, xb):
                    line(x)


def into(ref, lead=None):
    def put(x, ya, yb, lane, value):
        if lead is None:
            ref[x, ya:yb, :, lane : lane + C] = value
        else:
            ref[lead, x, ya:yb, :, lane : lane + C] = value

    return put


def product(get, weight):
    parts = []
    for a in range(3):
        for b in range(3):
            piece = get(a, b)
            parts.append(piece.reshape(-1, piece.shape[-1]))
    return jnp.dot(jnp.concatenate(parts, axis=1), weight[...], preferred_element_type=F32)


def band(weight, wide):
    wide[0 : 27 * C, 0:C] = weight[...]
    wide[9 * C : 36 * C, C : 2 * C] = weight[...]


def flip_kernel(first, second, first_out, second_out):
    for weight, out in ((second, second_out), (first, first_out)):

        def body(n, unused):
            for j in range(9):
                k = n * 9 + j
                block = weight[pl.ds(pl.multiple_of((26 - k) * C, C), C), :].T
                out[pl.ds(pl.multiple_of(k * C, C), C), :] = block
            return unused

        lax.fori_loop(0, 3, body, 0)


def clear_band(wide):
    wide[27 * C : 36 * C, 0:C] = jnp.zeros((9 * C, C), BF16)
    wide[0 : 9 * C, C : 2 * C] = jnp.zeros((9 * C, C), BF16)


def pairs(gets, wide):
    parts, sizes = [], None
    for j in range(4):
        for b in range(3):
            pieces = [get(j, b) for get in gets]
            pieces = [piece.reshape(-1, piece.shape[-1]) for piece in pieces]
            sizes = [piece.shape[0] for piece in pieces]
            parts.append(pieces[0] if len(pieces) == 1 else jnp.concatenate(pieces, axis=0))
    value = jnp.dot(jnp.concatenate(parts, axis=1), wide[...], preferred_element_type=F32)
    results, at = [], 0
    for size in sizes:
        results.append((value[at : at + size, 0:C], value[at : at + size, C : 2 * C]))
        at += size
    return results


def rounded(value):
    return value.astype(BF16).astype(F32)


def slope_of(value):
    sig = jax.nn.sigmoid(value)
    return sig * (1.0 + value * (1.0 - sig))


def live_rows(tab):
    parts = [
        jnp.where(tab[OWN, s * 27 + 13] < ZERO, jnp.ones((BE, C), F32), jnp.zeros((BE, C), F32))
        for s in range(NB)
    ]
    return jnp.concatenate(parts, axis=0)


def zero_slot(field):
    def body(x, unused):
        field[x, :, ZERO : ZERO + BE, :] = jnp.zeros((field.shape[1], BE, C), F32)
        return unused

    lax.fori_loop(0, field.shape[0], body, 0)


def rows_at(field, x, y, value):
    n, m = value.shape[:2]
    field[x : x + n, y : y + m, 0:ROWS, :] = value


def weight_grad(patch, grads, turned, out, which, scale):
    for x in range(BE):
        block = grads[x].reshape(BE * ROWS, C).T
        for a in range(3):
            at = (x + a) * BE * ROWS
            turned[a * C : (a + 1) * C, at : at + BE * ROWS] = block

    for b in range(3):
        right = patch[:, b : b + BE].reshape((BE + 2) * BE * ROWS, 3 * C)
        term = (jnp.dot(turned[...], right, preferred_element_type=F32) * scale).astype(BF16)
        for a in range(3):
            for c in range(3):
                at = (a * 9 + b * 3 + c) * C
                out[which, at : at + C, :] = term[a * C : (a + 1) * C, c * C : (c + 1) * C].T


def clear_turned(turned):
    width = BE * ROWS
    for a in range(3):
        for x in list(range(a)) + list(range(a + BE, BE + 2)):
            turned[a * C : (a + 1) * C, x * width : (x + 1) * width] = jnp.zeros((C, width), BF16)


def load_tables(lines, staged, tab, sem):
    for column, (ref, at) in lines.items():
        staged[column : column + 1, :] = ref[at, 0:16, :].astype(F32)[0:1].astype(jnp.int32)
    copy = pltpu.make_async_copy(staged, tab, sem)
    copy.start()
    copy.wait()


def first_payload_kernel(links, count, x, cot, xlow, xhigh, ylow, yhigh, own):
    lane = lax.broadcasted_iota(jnp.int32, (ROWS, C), 1)
    row = jnp.zeros((ROWS, C), jnp.int32)
    for s in range(NB):
        for d in range(27):
            if d == 13:
                named = jnp.where(s < count[0], s, -1)
            else:
                named = links[s, d if d < 13 else d - 1]
            start = jnp.where(named < 0, NB, named) * BE
            row = jnp.where(lane == s * 27 + d, start, row)
    line = row.astype(F32).astype(BF16)
    own[0] = line
    for ref, xa, xc in ((xlow, 0, 0), (xhigh, 5, 7)):
        ref[0:24] = x[xa : xa + 3].reshape(24, ROWS, C)
        ref[24:32] = cot[xc]
        ref[32] = line
    for ref, ya, yc in ((ylow, 0, 0), (yhigh, 5, 7)):
        for i in range(BE):
            ref[3 * i : 3 * i + 3] = x[i, ya : ya + 3]
        ref[24:32] = cot[:, yc]
        ref[32] = line


def corner_payload_kernel(xm, xp, low, high):
    for ref, ya, yc in ((low, 0, 0), (high, 5, 7)):
        for j, near in enumerate((xm, xp)):
            for i in range(3):
                ref[9 * j + 3 * i : 9 * j + 3 * i + 3] = near[8 * i + ya : 8 * i + ya + 3]
            ref[18 + j] = near[24 + yc]
            ref[20 + j] = near[32]


def edge_payload_kernel(xm, xp, b1, low, high):
    for ref, y in ((low, 0), (high, 7)):
        ref[0] = xm[y]
        ref[1:9] = b1[:, y]
        ref[9] = xp[y]


def main_kernel(scale, core, own, x, cot, xm, xp, ym, yp, qm, qp, w1, w2, w2f, out, b2o, b1o, elow, ehigh, gr,
                field, hid, back, p1, p2, px, py, pc, slope1, turned, wide, staged, tab, sem):
    load_tables(
        {0: (qm, 20), 1: (xm, 32), 2: (qp, 20), 3: (ym, 32), 4: (own, 0), 5: (yp, 32), 6: (qm, 21), 7: (xp, 32), 8: (qp, 21)},
        staged, tab, sem,
    )
    live = live_rows(tab)
    for ref in (field, hid, back):
        zero_slot(ref)
    clear_turned(turned)
    clear_band(wide)
    band(w1, wide)

    def fill(i, unused):
        field[3 + i, 3:11, 0:ROWS, :] = x[i].astype(F32)
        field[3 + i, 0:3, 0:ROWS, :] = ym[pl.ds(3 * i, 3)].astype(F32)
        field[3 + i, 11:14, 0:ROWS, :] = yp[pl.ds(3 * i, 3)].astype(F32)
        return unused

    lax.fori_loop(0, BE, fill, 0)
    for i in range(3):
        for at, near, q in ((i, xm, 3 * i), (11 + i, xp, 9 + 3 * i)):
            field[at, 3:11, 0:ROWS, :] = near[8 * i : 8 * i + 8].astype(F32)
            field[at, 0:3, 0:ROWS, :] = qm[q : q + 3].astype(F32)
            field[at, 11:14, 0:ROWS, :] = qp[q : q + 3].astype(F32)

    ends = spans(2)
    corners = [0, 2, 6, 8]
    build_patches(tab, field, into(p1), 3, OWN, ends[0], ends[0])
    for j, cx in enumerate((-1, 1)):
        build_patches(tab, field, into(px, j), 3, COLUMNS.index((cx, 0)), ends[cx], ends[0])
        build_patches(tab, field, into(py, j), 3, COLUMNS.index((0, cx)), ends[0], ends[cx])
    for j, c in enumerate(corners):
        build_patches(tab, field, into(pc, j), 3, c, ends[COLUMNS[c][0]], ends[COLUMNS[c][1]])

    def hide(pre):
        return rounded(pre * jax.nn.sigmoid(pre))

    def own_pairs(patch, i):
        results = pairs([lambda j, b, g=g: patch[4 * i + g + j, b : b + BE] for g in (0, 2)], wide)
        return [(4 * i + 2 * g + h, results[g][h].reshape(BE, ROWS, C)) for g in range(2) for h in range(2)]

    def y_pairs(m):
        gets = [lambda j, b, s=s, p=p: py[s, 2 * p + j, b : b + m] for s in range(2) for p in range(4)]
        results = pairs(gets, wide)
        return [
            (s, 2 * p + h, results[4 * s + p][h].reshape(m, ROWS, C)) for s in range(2) for p in range(4) for h in range(2)
        ]

    def first_own(i, unused):
        for at, pre in own_pairs(p1, i):
            slope1[at] = slope_of(pre)
            hid[2 + at, 2:10, 0:ROWS, :] = hide(pre)
        return unused

    lax.fori_loop(0, 2, first_own, 0)
    results = pairs([lambda j, b, s=s: px[s, j, b : b + BE] for s in range(2)], wide)
    for s in range(2):
        for h in range(2):
            hid[10 * s + h, 2:10, 0:ROWS, :] = hide(results[s][h]).reshape(BE, ROWS, C)
    for s, at, pre in y_pairs(2):
        hid[2 + at, 10 * s : 10 * s + 2, 0:ROWS, :] = hide(pre)
    [result] = pairs([lambda j, b: pc[:, j, b : b + 2]], wide)
    for h in range(2):
        value = hide(result[h]).reshape(4, 2, ROWS, C)
        for j, (ax, ay) in enumerate(((0, 0), (0, 10), (10, 0), (10, 10))):
            hid[ax + h, ay : ay + 2, 0:ROWS, :] = value[j]

    ends = spans(1)
    band(w2, wide)
    build_patches(tab, hid, into(p2), 2, OWN, ends[0], ends[0])
    for j, cx in enumerate((-1, 1)):
        build_patches(tab, hid, into(px, j), 2, COLUMNS.index((cx, 0)), ends[cx], ends[0])
        build_patches(tab, hid, into(py, j), 2, COLUMNS.index((0, cx)), ends[0], ends[cx])
    for j, c in enumerate(corners):
        build_patches(tab, hid, into(pc, j), 2, c, ends[COLUMNS[c][0]], ends[COLUMNS[c][1]])

    def second_own(i, unused):
        for at, pre in own_pairs(p2, i):
            total = field[3 + at, 3:11, 0:ROWS, :] * live + pre
            sig = jax.nn.sigmoid(total)
            out[at] = (total * sig * live).astype(BF16)
            slope = sig * (1.0 + total * (1.0 - sig))
            grad = (cot[at].astype(F32) * slope * live).astype(BF16)
            b2o[at] = grad
            back[1 + at, 1:9, 0:ROWS, :] = grad.astype(F32)
        return unused

    lax.fori_loop(0, 2, second_own, 0)
    for s, at, pre in y_pairs(1):
        near = (ym, yp)[s]
        total = field[3 + at, (2, 11)[s], 0:ROWS, :] + pre[0]
        back[1 + at, 9 * s, 0:ROWS, :] = rounded(near[24 + at].astype(F32) * slope_of(total))
    pre = product(lambda a, b: px[:, a : a + 1, b : b + BE], w2).reshape(2, BE, ROWS, C)
    for j, (at, cx, near) in enumerate(((2, 0, xm), (11, 9, xp))):
        total = field[at, 3:11, 0:ROWS, :] + pre[j]
        back[cx, 1:9, 0:ROWS, :] = rounded(near[24:32].astype(F32) * slope_of(total))
    pre = product(lambda a, b: pc[:, a : a + 1, b : b + 1], w2).reshape(4, ROWS, C)
    for j, (ax, ay, cx, cy, near, at) in enumerate(
        ((2, 2, 0, 0, qm, 18), (2, 11, 0, 9, qp, 18), (11, 2, 9, 0, qm, 19), (11, 11, 9, 9, qp, 19))
    ):
        total = field[ax, ay, 0:ROWS, :] + pre[j]
        back[cx, cy, 0:ROWS, :] = rounded(near[at].astype(F32) * slope_of(total))
    weight_grad(p2, b2o, turned, gr, 1 - core[0], scale)

    band(w2f, wide)
    build_patches(tab, back, into(p2), 1, OWN, (0, BE), (0, BE))

    def third(i, unused):
        for at, pre in own_pairs(p2, i):
            b1o[at] = (pre * slope1[at] * live).astype(BF16)
        return unused

    lax.fori_loop(0, 2, third, 0)
    elow[...] = b1o[0]
    ehigh[...] = b1o[7]
    weight_grad(p1, b1o, turned, gr, core[0], scale)


def last_kernel(own, b1, b2, xm, xp, ym, yp, w1f, out, field, patch, wide, staged, tab, sem):
    load_tables({OWN: (own, 0)}, staged, tab, sem)
    live = live_rows(tab)
    zero_slot(field)
    clear_band(wide)
    band(w1f, wide)

    def fill(i, unused):
        field[1 + i, 1:9, 0:ROWS, :] = b1[i].astype(F32)
        return unused

    lax.fori_loop(0, BE, fill, 0)
    field[0, 1:9, 0:ROWS, :] = xm[...].astype(F32)
    field[9, 1:9, 0:ROWS, :] = xp[...].astype(F32)
    field[:, 0, 0:ROWS, :] = ym[...].astype(F32)
    field[:, 9, 0:ROWS, :] = yp[...].astype(F32)
    build_patches(tab, field, into(patch), 1, OWN, (0, BE), (0, BE))

    def step(i, unused):
        results = pairs([lambda j, b, g=g: patch[4 * i + g + j, b : b + BE] for g in (0, 2)], wide)
        for g in range(2):
            for h in range(2):
                at = 4 * i + 2 * g + h
                out[at] = ((b2[at].astype(F32) + results[g][h].reshape(BE, ROWS, C)) * live).astype(BF16)
        return unused

    lax.fori_loop(0, 2, step, 0)


def call(kernel, outs, scratch, cost, mib, scalars, *args):
    smem = pl.BlockSpec(memory_space=pltpu.SMEM)
    vmem = pl.BlockSpec(memory_space=pltpu.VMEM)
    return pl.pallas_call(
        kernel,
        out_shape=outs,
        in_specs=[smem] * scalars + [vmem] * (len(args) - scalars),
        out_specs=jax.tree.map(lambda o: vmem, outs),
        scratch_shapes=scratch,
        compiler_params=pltpu.CompilerParams(vmem_limit_bytes=mib * 2**20),
        cost_estimate=pl.CostEstimate(flops=cost[0], bytes_accessed=cost[1], transcendentals=0),
    )(*args)


def swap_cores(part):
    return lax.ppermute(part, "dp", [(0, 1), (1, 0)])


def sum_scatter(part, axis):
    n = lax.axis_size(axis)
    swapped = lax.all_to_all(part.reshape(n, part.shape[0] // n, C), axis, 0, 0, tiled=True)
    return jnp.sum(swapped.astype(F32), axis=0).astype(BF16)


def sum_pairs(part, axis):
    n = lax.axis_size(axis)
    reach = 1
    while reach < n:
        other = lax.ppermute(part, axis, [(i, i ^ (2 * reach - 1)) for i in range(n)])
        part = (part.astype(F32) + other.astype(F32)).astype(BF16)
        reach *= 2
    return part


def gather_axis(part, axis):
    n = lax.axis_size(axis)
    copies = jnp.broadcast_to(part[None], (n,) + part.shape)
    return lax.all_to_all(copies, axis, 0, 0, tiled=True).reshape(n * part.shape[0], C)


def shape_of(*sizes):
    return jax.ShapeDtypeStruct(sizes, BF16)


def shards(features, cotangent, first_weight, second_weight, neighbours, counts):
    x = features.reshape(BE, BE, ROWS, C)
    cot = cotangent.reshape(BE, BE, ROWS, C)
    w1, w2 = first_weight.reshape(27 * C, C), second_weight.reshape(27 * C, C)
    n_devices = lax.axis_size("sx") * lax.axis_size("sy") * lax.axis_size("dp")
    scale = float(n_devices * NB * BE**3) ** -0.5
    core = lax.axis_index("dp").astype(jnp.int32)

    payload = shape_of(33, ROWS, C)
    xlow, xhigh, ylow, yhigh, own = call(
        first_payload_kernel, [payload] * 4 + [shape_of(1, ROWS, C)], [], (0, 2**21), 8, 2,
        neighbours.reshape(NB, 26), counts.reshape(1), x, cot,
    )
    xm, xp = shift_pair(xlow, xhigh, "sx")
    ym, yp = shift_pair(ylow, yhigh, "sy")
    qlow, qhigh = call(corner_payload_kernel, [shape_of(22, ROWS, C)] * 2, [], (0, 2**19), 8, 0, xm, xp)
    held1, held2, qlow, qhigh = lax.optimization_barrier((w1, w2, qlow, qhigh))
    qm, qp = shift_pair(qlow, qhigh, "sy")
    w1f, w2f = call(flip_kernel, [shape_of(27 * C, C)] * 2, [], (2**24, 2**22), 8, 0, held1, held2)

    block, edge = shape_of(BE, BE, ROWS, C), shape_of(BE, ROWS, C)
    lanes = 3 * C
    unit = 2 * BE * BE * ROWS * 27 * C * C
    tables = [pltpu.VMEM((16, C), jnp.int32), pltpu.SMEM((16, C), jnp.int32), pltpu.SemaphoreType.DMA]
    out, b2, b1, elow, ehigh, grads = call(
        functools.partial(main_kernel, scale),
        [block, block, block, edge, edge, shape_of(2, 27 * C, C)],
        [
            pltpu.VMEM((14, 14, ROWS + BE, C), F32),
            pltpu.VMEM((12, 12, ROWS + BE, C), F32),
            pltpu.VMEM((10, 10, ROWS + BE, C), F32),
            pltpu.VMEM((10, 10, ROWS, lanes), BF16),
            pltpu.VMEM((10, 10, ROWS, lanes), BF16),
            pltpu.VMEM((2, 4, 10, ROWS, lanes), BF16),
            pltpu.VMEM((2, 10, 4, ROWS, lanes), BF16),
            pltpu.VMEM((4, 4, 4, ROWS, lanes), BF16),
            pltpu.VMEM((BE, BE, ROWS, C), F32),
            pltpu.VMEM((3 * C, (BE + 2) * BE * ROWS), BF16),
            pltpu.VMEM((36 * C, 2 * C), BF16),
            *tables,
        ],
        (7 * unit, 10 * 2**20), 32, 1,
        core.reshape(1), own, x, cot, xm, xp, ym, yp, qm, qp, w1, w2, w2f,
    )

    received = swap_cores(grads[1])
    bxm, bxp = shift_pair(elow, ehigh, "sx")
    part = (grads[0].astype(F32) + received.astype(F32)).astype(BF16)
    blow, bhigh = call(edge_payload_kernel, [shape_of(BE + 2, ROWS, C)] * 2, [], (0, 2**19), 8, 0, bxm, bxp, b1)
    part, blow, bhigh = lax.optimization_barrier((part, blow, bhigh))
    bym, byp = shift_pair(blow, bhigh, "sy")
    part, bym, byp = lax.optimization_barrier((sum_scatter(part, "sy"), bym, byp))
    part, b2 = lax.optimization_barrier((sum_pairs(part, "sx"), b2))

    grad_input = call(
        last_kernel,
        block,
        [
            pltpu.VMEM((10, 10, ROWS + BE, C), F32),
            pltpu.VMEM((10, 10, ROWS, lanes), BF16),
            pltpu.VMEM((36 * C, 2 * C), BF16),
            *tables,
        ],
        (unit, 4 * 2**20), 12, 0,
        own, b1, b2, bxm, bxp, bym, byp, w1f,
    )
    part, grad_input = lax.optimization_barrier((gather_axis(part, "sy"), grad_input))
    other = swap_cores(part)
    first = jnp.where(core == 0, part, other).astype(F32).reshape(27, C, C)
    second = jnp.where(core == 0, other, part).astype(F32).reshape(27, C, C)
    shape = features.shape
    return out.reshape(shape), grad_input.reshape(shape), first, second


def solution(mesh):
    column = P("dp", "sx", "sy", None, None, None)
    return jax.shard_map(
        shards,
        mesh=mesh,
        in_specs=(column, column, P(), P(), P("dp", "sx", "sy", None, None), P("dp", "sx", "sy")),
        out_specs=(column, column, P(), P()),
        check_vma=False,
    )
```

```python
import functools

import jax
import jax.numpy as jnp
from jax import lax
from jax.experimental import pallas as pl
from jax.experimental.pallas import tpu as pltpu
from jax.sharding import PartitionSpec as P

C = 128
BE = 8
NB = 4
ROWS = NB * BE
ZERO = ROWS
F32 = jnp.float32
BF16 = jnp.bfloat16
COLUMNS = [(cx, cy) for cx in (-1, 0, 1) for cy in (-1, 0, 1)]
OWN = 4


def shift_pair(low, high, axis):
    n = lax.axis_size(axis)
    from_low = lax.ppermute(high, axis, [(i, (i + 1) % n) for i in range(n)])
    from_high = lax.ppermute(low, axis, [((i + 1) % n, i) for i in range(n)])
    return from_low, from_high


def spans(halo):
    return {-1: (0, halo), 0: (halo, halo + BE), 1: (halo + BE, 2 * halo + BE)}


def build_patches(tab, field, put, halo, column, xs, ys):
    cx, cy = COLUMNS[column]
    row = lax.broadcasted_iota(jnp.int32, (1, BE, C), 1)
    for sx, (x0, x1) in spans(halo).items():
        xa, xb = max(x0, xs[0]), min(x1, xs[1] + 2)
        if xa >= xb:
            continue
        for sy, (y0, y1) in spans(halo).items():
            ya, yb = max(y0, ys[0]), min(y1, ys[1] + 2)
            if ya >= yb:
                continue
            first = (sx - cx + 1) * 9 + (sy - cy + 1) * 3
            offsets = [
                [pl.multiple_of(tab[column, s * 27 + first + j], BE) for j in range(3)]
                for s in range(NB)
            ]

            def line(x):
                parts = [[], [], []]
                for below, here, above in offsets:
                    v = field[x, ya:yb, pl.ds(here, BE), :]
                    lo = field[x, ya:yb, pl.ds(below, BE), :]
                    hi = field[x, ya:yb, pl.ds(above, BE), :]
                    parts[0].append(pltpu.roll(jnp.where(row == BE - 1, lo, v), 1, 1))
                    parts[1].append(v)
                    parts[2].append(pltpu.roll(jnp.where(row == 0, hi, v), BE - 1, 1))
                for j in range(3):
                    value = jnp.concatenate(parts[j], axis=1).astype(BF16)
                    put(x - xs[0], ya - ys[0], yb - ys[0], j * C, value)

            if xb - xa > 3:

                def body(x, unused):
                    line(x)
                    return unused

                lax.fori_loop(xa, xb, body, 0)
            else:
                for x in range(xa, xb):
                    line(x)


def into(ref, lead=None):
    def put(x, ya, yb, lane, value):
        if lead is None:
            ref[x, ya:yb, :, lane : lane + C] = value
        else:
            ref[lead, x, ya:yb, :, lane : lane + C] = value

    return put


def product(get, weight):
    parts = []
    for a in range(3):
        for b in range(3):
            piece = get(a, b)
            parts.append(piece.reshape(-1, piece.shape[-1]))
    return jnp.dot(jnp.concatenate(parts, axis=1), weight[...], preferred_element_type=F32)


def band(weight, wide):
    wide[0 : 27 * C, 0:C] = weight[...]
    wide[9 * C : 36 * C, C : 2 * C] = weight[...]


def flip_kernel(first, second, first_out, second_out):
    for weight, out in ((second, second_out), (first, first_out)):

        def body(n, unused):
            for j in range(9):
                k = n * 9 + j
                block = weight[pl.ds(pl.multiple_of((26 - k) * C, C), C), :].T
                out[pl.ds(pl.multiple_of(k * C, C), C), :] = block
            return unused

        lax.fori_loop(0, 3, body, 0)


def clear_band(wide):
    wide[27 * C : 36 * C, 0:C] = jnp.zeros((9 * C, C), BF16)
    wide[0 : 9 * C, C : 2 * C] = jnp.zeros((9 * C, C), BF16)


def pairs(gets, wide):
    parts, sizes = [], None
    for j in range(4):
        for b in range(3):
            pieces = [get(j, b) for get in gets]
            pieces = [piece.reshape(-1, piece.shape[-1]) for piece in pieces]
            sizes = [piece.shape[0] for piece in pieces]
            parts.append(pieces[0] if len(pieces) == 1 else jnp.concatenate(pieces, axis=0))
    value = jnp.dot(jnp.concatenate(parts, axis=1), wide[...], preferred_element_type=F32)
    results, at = [], 0
    for size in sizes:
        results.append((value[at : at + size, 0:C], value[at : at + size, C : 2 * C]))
        at += size
    return results


def rounded(value):
    return value.astype(BF16).astype(F32)


def slope_of(value):
    sig = jax.nn.sigmoid(value)
    return sig * (1.0 + value * (1.0 - sig))


def live_rows(tab):
    parts = [
        jnp.where(tab[OWN, s * 27 + 13] < ZERO, jnp.ones((BE, C), F32), jnp.zeros((BE, C), F32))
        for s in range(NB)
    ]
    return jnp.concatenate(parts, axis=0)


def zero_slot(field):
    def body(x, unused):
        field[x, :, ZERO : ZERO + BE, :] = jnp.zeros((field.shape[1], BE, C), F32)
        return unused

    lax.fori_loop(0, field.shape[0], body, 0)


def rows_at(field, x, y, value):
    n, m = value.shape[:2]
    field[x : x + n, y : y + m, 0:ROWS, :] = value


def weight_grad(patch, grads, turned, out, which, scale):
    for x in range(BE):
        block = grads[x].reshape(BE * ROWS, C).T
        for a in range(3):
            at = (x + a) * BE * ROWS
            turned[a * C : (a + 1) * C, at : at + BE * ROWS] = block

    for b in range(3):
        right = patch[:, b : b + BE].reshape((BE + 2) * BE * ROWS, 3 * C)
        term = (jnp.dot(turned[...], right, preferred_element_type=F32) * scale).astype(BF16)
        for a in range(3):
            for c in range(3):
                at = (a * 9 + b * 3 + c) * C
                out[which, at : at + C, :] = term[a * C : (a + 1) * C, c * C : (c + 1) * C].T


def clear_turned(turned):
    width = BE * ROWS
    for a in range(3):
        for x in list(range(a)) + list(range(a + BE, BE + 2)):
            turned[a * C : (a + 1) * C, x * width : (x + 1) * width] = jnp.zeros((C, width), BF16)


def load_tables(lines, staged, tab, sem):
    for column, (ref, at) in lines.items():
        staged[column : column + 1, :] = ref[at, 0:16, :].astype(F32)[0:1].astype(jnp.int32)
    copy = pltpu.make_async_copy(staged, tab, sem)
    copy.start()
    copy.wait()


def first_payload_kernel(links, count, x_far, cot_far, xlow, xhigh, ylow, yhigh, own, x, cot, sems):
    copies = [pltpu.make_async_copy(x_far, x, sems.at[0]), pltpu.make_async_copy(cot_far, cot, sems.at[1])]
    for copy in copies:
        copy.start()
    lane = lax.broadcasted_iota(jnp.int32, (ROWS, C), 1)
    row = jnp.zeros((ROWS, C), jnp.int32)
    for s in range(NB):
        for d in range(27):
            if d == 13:
                named = jnp.where(s < count[0], s, -1)
            else:
                named = links[s, d if d < 13 else d - 1]
            start = jnp.where(named < 0, NB, named) * BE
            row = jnp.where(lane == s * 27 + d, start, row)
    line = row.astype(F32).astype(BF16)
    own[0] = line
    for copy in copies:
        copy.wait()
    for ref, xa, xc in ((xlow, 0, 0), (xhigh, 5, 7)):
        ref[0:24] = x[xa : xa + 3].reshape(24, ROWS, C)
        ref[24:32] = cot[xc]
        ref[32] = line
    for ref, ya, yc in ((ylow, 0, 0), (yhigh, 5, 7)):
        for i in range(BE):
            ref[3 * i : 3 * i + 3] = x[i, ya : ya + 3]
        ref[24:32] = cot[:, yc]
        ref[32] = line


def corner_payload_kernel(xm, xp, low, high):
    for ref, ya, yc in ((low, 0, 0), (high, 5, 7)):
        for j, near in enumerate((xm, xp)):
            for i in range(3):
                ref[9 * j + 3 * i : 9 * j + 3 * i + 3] = near[8 * i + ya : 8 * i + ya + 3]
            ref[18 + j] = near[24 + yc]
            ref[20 + j] = near[32]


def edge_payload_kernel(xm, xp, b1, low, high):
    for ref, y in ((low, 0), (high, 7)):
        ref[0] = xm[y]
        ref[1:9] = b1[:, y]
        ref[9] = xp[y]


def main_kernel(scale, core, *refs):
    far, own, refs = refs[:11], refs[11], refs[12:]
    out, b2o, b1o, elow, ehigh, gr = refs[:6]
    near, (sems, field, hid, back, p1, p2, px, py, pc, slope1, turned, wide, staged, tab, sem) = refs[6:17], refs[17:]
    x, cot, xm, xp, ym, yp, qm, qp, w1, w2, w2f = near
    copies = [pltpu.make_async_copy(far[i], near[i], sems.at[i]) for i in range(11)]
    order = [8, 0, 2, 3, 4, 5, 6, 7, 1, 9, 10]
    for i in order:
        copies[i].start()
    for ref in (field, hid, back):
        zero_slot(ref)
    clear_turned(turned)
    clear_band(wide)
    copies[8].wait()
    band(w1, wide)
    for i in order[1:8]:
        copies[i].wait()
    load_tables(
        {0: (qm, 20), 1: (xm, 32), 2: (qp, 20), 3: (ym, 32), 4: (own, 0), 5: (yp, 32), 6: (qm, 21), 7: (xp, 32), 8: (qp, 21)},
        staged, tab, sem,
    )
    live = live_rows(tab)

    def fill(i, unused):
        field[3 + i, 3:11, 0:ROWS, :] = x[i].astype(F32)
        field[3 + i, 0:3, 0:ROWS, :] = ym[pl.ds(3 * i, 3)].astype(F32)
        field[3 + i, 11:14, 0:ROWS, :] = yp[pl.ds(3 * i, 3)].astype(F32)
        return unused

    lax.fori_loop(0, BE, fill, 0)
    for i in range(3):
        for at, near, q in ((i, xm, 3 * i), (11 + i, xp, 9 + 3 * i)):
            field[at, 3:11, 0:ROWS, :] = near[8 * i : 8 * i + 8].astype(F32)
            field[at, 0:3, 0:ROWS, :] = qm[q : q + 3].astype(F32)
            field[at, 11:14, 0:ROWS, :] = qp[q : q + 3].astype(F32)

    ends = spans(2)
    corners = [0, 2, 6, 8]
    build_patches(tab, field, into(p1), 3, OWN, ends[0], ends[0])
    for j, cx in enumerate((-1, 1)):
        build_patches(tab, field, into(px, j), 3, COLUMNS.index((cx, 0)), ends[cx], ends[0])
        build_patches(tab, field, into(py, j), 3, COLUMNS.index((0, cx)), ends[0], ends[cx])
    for j, c in enumerate(corners):
        build_patches(tab, field, into(pc, j), 3, c, ends[COLUMNS[c][0]], ends[COLUMNS[c][1]])

    def hide(pre):
        return rounded(pre * jax.nn.sigmoid(pre))

    def own_pairs(patch, i):
        results = pairs([lambda j, b, g=g: patch[4 * i + g + j, b : b + BE] for g in (0, 2)], wide)
        return [(4 * i + 2 * g + h, results[g][h].reshape(BE, ROWS, C)) for g in range(2) for h in range(2)]

    def y_pairs(m):
        gets = [lambda j, b, s=s, p=p: py[s, 2 * p + j, b : b + m] for s in range(2) for p in range(4)]
        results = pairs(gets, wide)
        return [
            (s, 2 * p + h, results[4 * s + p][h].reshape(m, ROWS, C)) for s in range(2) for p in range(4) for h in range(2)
        ]

    def first_own(i, unused):
        for at, pre in own_pairs(p1, i):
            slope1[at] = slope_of(pre)
            hid[2 + at, 2:10, 0:ROWS, :] = hide(pre)
        return unused

    lax.fori_loop(0, 2, first_own, 0)
    results = pairs([lambda j, b, s=s: px[s, j, b : b + BE] for s in range(2)], wide)
    for s in range(2):
        for h in range(2):
            hid[10 * s + h, 2:10, 0:ROWS, :] = hide(results[s][h]).reshape(BE, ROWS, C)
    for s, at, pre in y_pairs(2):
        hid[2 + at, 10 * s : 10 * s + 2, 0:ROWS, :] = hide(pre)
    [result] = pairs([lambda j, b: pc[:, j, b : b + 2]], wide)
    for h in range(2):
        value = hide(result[h]).reshape(4, 2, ROWS, C)
        for j, (ax, ay) in enumerate(((0, 0), (0, 10), (10, 0), (10, 10))):
            hid[ax + h, ay : ay + 2, 0:ROWS, :] = value[j]

    ends = spans(1)
    for i in order[8:]:
        copies[i].wait()
    band(w2, wide)
    build_patches(tab, hid, into(p2), 2, OWN, ends[0], ends[0])
    for j, cx in enumerate((-1, 1)):
        build_patches(tab, hid, into(px, j), 2, COLUMNS.index((cx, 0)), ends[cx], ends[0])
        build_patches(tab, hid, into(py, j), 2, COLUMNS.index((0, cx)), ends[0], ends[cx])
    for j, c in enumerate(corners):
        build_patches(tab, hid, into(pc, j), 2, c, ends[COLUMNS[c][0]], ends[COLUMNS[c][1]])

    def second_own(i, unused):
        for at, pre in own_pairs(p2, i):
            total = field[3 + at, 3:11, 0:ROWS, :] * live + pre
            sig = jax.nn.sigmoid(total)
            out[at] = (total * sig * live).astype(BF16)
            slope = sig * (1.0 + total * (1.0 - sig))
            grad = (cot[at].astype(F32) * slope * live).astype(BF16)
            b2o[at] = grad
            back[1 + at, 1:9, 0:ROWS, :] = grad.astype(F32)
        return unused

    lax.fori_loop(0, 2, second_own, 0)
    for s, at, pre in y_pairs(1):
        near = (ym, yp)[s]
        total = field[3 + at, (2, 11)[s], 0:ROWS, :] + pre[0]
        back[1 + at, 9 * s, 0:ROWS, :] = rounded(near[24 + at].astype(F32) * slope_of(total))
    pre = product(lambda a, b: px[:, a : a + 1, b : b + BE], w2).reshape(2, BE, ROWS, C)
    for j, (at, cx, near) in enumerate(((2, 0, xm), (11, 9, xp))):
        total = field[at, 3:11, 0:ROWS, :] + pre[j]
        back[cx, 1:9, 0:ROWS, :] = rounded(near[24:32].astype(F32) * slope_of(total))
    pre = product(lambda a, b: pc[:, a : a + 1, b : b + 1], w2).reshape(4, ROWS, C)
    for j, (ax, ay, cx, cy, near, at) in enumerate(
        ((2, 2, 0, 0, qm, 18), (2, 11, 0, 9, qp, 18), (11, 2, 9, 0, qm, 19), (11, 11, 9, 9, qp, 19))
    ):
        total = field[ax, ay, 0:ROWS, :] + pre[j]
        back[cx, cy, 0:ROWS, :] = rounded(near[at].astype(F32) * slope_of(total))
    weight_grad(p2, b2o, turned, gr, 1 - core[0], scale)

    band(w2f, wide)
    build_patches(tab, back, into(p2), 1, OWN, (0, BE), (0, BE))

    def third(i, unused):
        for at, pre in own_pairs(p2, i):
            b1o[at] = (pre * slope1[at] * live).astype(BF16)
        return unused

    lax.fori_loop(0, 2, third, 0)
    elow[...] = b1o[0]
    ehigh[...] = b1o[7]
    weight_grad(p1, b1o, turned, gr, core[0], scale)


def last_kernel(own, b1, b2, xm, xp, ym, yp, w1f, out, field, patch, wide, staged, tab, sem):
    load_tables({OWN: (own, 0)}, staged, tab, sem)
    live = live_rows(tab)
    zero_slot(field)
    clear_band(wide)
    band(w1f, wide)

    def fill(i, unused):
        field[1 + i, 1:9, 0:ROWS, :] = b1[i].astype(F32)
        return unused

    lax.fori_loop(0, BE, fill, 0)
    field[0, 1:9, 0:ROWS, :] = xm[...].astype(F32)
    field[9, 1:9, 0:ROWS, :] = xp[...].astype(F32)
    field[:, 0, 0:ROWS, :] = ym[...].astype(F32)
    field[:, 9, 0:ROWS, :] = yp[...].astype(F32)
    build_patches(tab, field, into(patch), 1, OWN, (0, BE), (0, BE))

    def step(i, unused):
        results = pairs([lambda j, b, g=g: patch[4 * i + g + j, b : b + BE] for g in (0, 2)], wide)
        for g in range(2):
            for h in range(2):
                at = 4 * i + 2 * g + h
                out[at] = ((b2[at].astype(F32) + results[g][h].reshape(BE, ROWS, C)) * live).astype(BF16)
        return unused

    lax.fori_loop(0, 2, step, 0)


def call(kernel, outs, scratch, cost, mib, scalars, far, *args):
    smem = pl.BlockSpec(memory_space=pltpu.SMEM)
    vmem = pl.BlockSpec(memory_space=pltpu.VMEM)
    anywhere = pl.BlockSpec(memory_space=pltpu.HBM)
    args = [
        pltpu.with_memory_space_constraint(arg, pltpu.HBM) if scalars <= i < scalars + far else arg
        for i, arg in enumerate(args)
    ]
    return pl.pallas_call(
        kernel,
        out_shape=outs,
        in_specs=[smem] * scalars + [anywhere] * far + [vmem] * (len(args) - scalars - far),
        out_specs=jax.tree.map(lambda o: vmem, outs),
        scratch_shapes=scratch,
        compiler_params=pltpu.CompilerParams(vmem_limit_bytes=mib * 2**20),
        cost_estimate=pl.CostEstimate(flops=cost[0], bytes_accessed=cost[1], transcendentals=0),
    )(*args)


def swap_cores(part):
    return lax.ppermute(part, "dp", [(0, 1), (1, 0)])


def sum_scatter(part, axis):
    n = lax.axis_size(axis)
    swapped = lax.all_to_all(part.reshape(n, part.shape[0] // n, C), axis, 0, 0, tiled=True)
    return jnp.sum(swapped.astype(F32), axis=0).astype(BF16)


def sum_pairs(part, axis):
    n = lax.axis_size(axis)
    reach = 1
    while reach < n:
        other = lax.ppermute(part, axis, [(i, i ^ (2 * reach - 1)) for i in range(n)])
        part = (part.astype(F32) + other.astype(F32)).astype(BF16)
        reach *= 2
    return part


def gather_axis(part, axis):
    n = lax.axis_size(axis)
    copies = jnp.broadcast_to(part[None], (n,) + part.shape)
    return lax.all_to_all(copies, axis, 0, 0, tiled=True).reshape(n * part.shape[0], C)


def shape_of(*sizes):
    return jax.ShapeDtypeStruct(sizes, BF16)


def shards(features, cotangent, first_weight, second_weight, neighbours, counts):
    x = features.reshape(BE, BE, ROWS, C)
    cot = cotangent.reshape(BE, BE, ROWS, C)
    w1, w2 = first_weight.reshape(27 * C, C), second_weight.reshape(27 * C, C)
    n_devices = lax.axis_size("sx") * lax.axis_size("sy") * lax.axis_size("dp")
    scale = float(n_devices * NB * BE**3) ** -0.5
    core = lax.axis_index("dp").astype(jnp.int32)

    payload = shape_of(33, ROWS, C)
    xlow, xhigh, ylow, yhigh, own = call(
        first_payload_kernel, [payload] * 4 + [shape_of(1, ROWS, C)],
        [pltpu.VMEM((BE, BE, ROWS, C), BF16)] * 2 + [pltpu.SemaphoreType.DMA((2,))], (0, 2**21), 8, 2, 2,
        neighbours.reshape(NB, 26), counts.reshape(1), x, cot,
    )
    xm, xp = shift_pair(xlow, xhigh, "sx")
    ym, yp = shift_pair(ylow, yhigh, "sy")
    qlow, qhigh = call(corner_payload_kernel, [shape_of(22, ROWS, C)] * 2, [], (0, 2**19), 8, 0, 0, xm, xp)
    held1, held2, qlow, qhigh = lax.optimization_barrier((w1, w2, qlow, qhigh))
    qm, qp = shift_pair(qlow, qhigh, "sy")
    w1f, w2f = call(flip_kernel, [shape_of(27 * C, C)] * 2, [], (2**24, 2**22), 8, 0, 0, held1, held2)

    block, edge = shape_of(BE, BE, ROWS, C), shape_of(BE, ROWS, C)
    lanes = 3 * C
    unit = 2 * BE * BE * ROWS * 27 * C * C
    tables = [pltpu.VMEM((16, C), jnp.int32), pltpu.SMEM((16, C), jnp.int32), pltpu.SemaphoreType.DMA]
    out, b2, b1, elow, ehigh, grads = call(
        functools.partial(main_kernel, scale),
        [block, block, block, edge, edge, shape_of(2, 27 * C, C)],
        [
            *[pltpu.VMEM((BE, BE, ROWS, C), BF16)] * 2,
            *[pltpu.VMEM((33, ROWS, C), BF16)] * 4,
            *[pltpu.VMEM((22, ROWS, C), BF16)] * 2,
            *[pltpu.VMEM((27 * C, C), BF16)] * 3,
            pltpu.SemaphoreType.DMA((11,)),
            pltpu.VMEM((14, 14, ROWS + BE, C), F32),
            pltpu.VMEM((12, 12, ROWS + BE, C), F32),
            pltpu.VMEM((10, 10, ROWS + BE, C), F32),
            pltpu.VMEM((10, 10, ROWS, lanes), BF16),
            pltpu.VMEM((10, 10, ROWS, lanes), BF16),
            pltpu.VMEM((2, 4, 10, ROWS, lanes), BF16),
            pltpu.VMEM((2, 10, 4, ROWS, lanes), BF16),
            pltpu.VMEM((4, 4, 4, ROWS, lanes), BF16),
            pltpu.VMEM((BE, BE, ROWS, C), F32),
            pltpu.VMEM((3 * C, (BE + 2) * BE * ROWS), BF16),
            pltpu.VMEM((36 * C, 2 * C), BF16),
            *tables,
        ],
        (7 * unit, 10 * 2**20), 40, 1, 11,
        core.reshape(1), x, cot, xm, xp, ym, yp, qm, qp, w1, w2, w2f, own,
    )

    received = swap_cores(grads[1])
    bxm, bxp = shift_pair(elow, ehigh, "sx")
    part = (grads[0].astype(F32) + received.astype(F32)).astype(BF16)
    part, bxm, bxp = lax.optimization_barrier((sum_scatter(part, "sy"), bxm, bxp))
    blow, bhigh = call(edge_payload_kernel, [shape_of(BE + 2, ROWS, C)] * 2, [], (0, 2**19), 8, 0, 0, bxm, bxp, b1)
    bym, byp = shift_pair(blow, bhigh, "sy")
    part, bym, byp, b2 = lax.optimization_barrier((sum_pairs(part, "sx"), bym, byp, b2))

    grad_input = call(
        last_kernel,
        block,
        [
            pltpu.VMEM((10, 10, ROWS + BE, C), F32),
            pltpu.VMEM((10, 10, ROWS, lanes), BF16),
            pltpu.VMEM((36 * C, 2 * C), BF16),
            *tables,
        ],
        (unit, 4 * 2**20), 12, 0, 0,
        own, b1, b2, bxm, bxp, bym, byp, w1f,
    )
    part, grad_input = lax.optimization_barrier((gather_axis(part, "sy"), grad_input))
    part = part.reshape(27, C, C)
    other = swap_cores(part)
    first = jnp.where(core == 0, part, other).astype(F32)
    second = jnp.where(core == 0, other, part).astype(F32)
    shape = features.shape
    return out.reshape(shape), grad_input.reshape(shape), first, second


def solution(mesh):
    column = P("dp", "sx", "sy", None, None, None)
    return jax.shard_map(
        shards,
        mesh=mesh,
        in_specs=(column, column, P(), P(), P("dp", "sx", "sy", None, None), P("dp", "sx", "sy")),
        out_specs=(column, column, P(), P()),
        check_vma=False,
    )
```

```python
import functools

import jax
import jax.numpy as jnp
from jax import lax
from jax.experimental import pallas as pl
from jax.experimental.pallas import tpu as pltpu
from jax.sharding import PartitionSpec as P

C = 128
BE = 8
NB = 4
ROWS = NB * BE
ZERO = ROWS
F32 = jnp.float32
BF16 = jnp.bfloat16
COLUMNS = [(cx, cy) for cx in (-1, 0, 1) for cy in (-1, 0, 1)]
OWN = 4


def shift_pair(low, high, axis):
    n = lax.axis_size(axis)
    from_low = lax.ppermute(high, axis, [(i, (i + 1) % n) for i in range(n)])
    from_high = lax.ppermute(low, axis, [((i + 1) % n, i) for i in range(n)])
    return from_low, from_high


def spans(halo):
    return {-1: (0, halo), 0: (halo, halo + BE), 1: (halo + BE, 2 * halo + BE)}


def build_patches(tab, field, put, halo, column, xs, ys):
    cx, cy = COLUMNS[column]
    row = lax.broadcasted_iota(jnp.int32, (1, BE, C), 1)
    for sx, (x0, x1) in spans(halo).items():
        xa, xb = max(x0, xs[0]), min(x1, xs[1] + 2)
        if xa >= xb:
            continue
        for sy, (y0, y1) in spans(halo).items():
            ya, yb = max(y0, ys[0]), min(y1, ys[1] + 2)
            if ya >= yb:
                continue
            first = (sx - cx + 1) * 9 + (sy - cy + 1) * 3
            offsets = [
                [pl.multiple_of(tab[column, s * 27 + first + j], BE) for j in range(3)]
                for s in range(NB)
            ]

            def line(x):
                parts = [[], [], []]
                for below, here, above in offsets:
                    v = field[x, ya:yb, pl.ds(here, BE), :]
                    lo = field[x, ya:yb, pl.ds(below, BE), :]
                    hi = field[x, ya:yb, pl.ds(above, BE), :]
                    parts[0].append(pltpu.roll(jnp.where(row == BE - 1, lo, v), 1, 1))
                    parts[1].append(v)
                    parts[2].append(pltpu.roll(jnp.where(row == 0, hi, v), BE - 1, 1))
                for j in range(3):
                    value = jnp.concatenate(parts[j], axis=1).astype(BF16)
                    put(x - xs[0], ya - ys[0], yb - ys[0], j * C, value)

            if xb - xa > 8:

                def body(x, unused):
                    line(x)
                    return unused

                lax.fori_loop(xa, xb, body, 0)
            else:
                for x in range(xa, xb):
                    line(x)


def into(ref, lead=None):
    def put(x, ya, yb, lane, value):
        if lead is None:
            ref[x, ya:yb, :, lane : lane + C] = value
        else:
            ref[lead, x, ya:yb, :, lane : lane + C] = value

    return put


def product(get, weight):
    parts = []
    for a in range(3):
        for b in range(3):
            piece = get(a, b)
            parts.append(piece.reshape(-1, piece.shape[-1]))
    return jnp.dot(jnp.concatenate(parts, axis=1), weight[...], preferred_element_type=F32)


def band(weight, wide):
    wide[0 : 27 * C, 0:C] = weight[...]
    wide[9 * C : 36 * C, C : 2 * C] = weight[...]


def flip_kernel(first, second, first_out, second_out):
    for weight, out in ((second, second_out), (first, first_out)):

        def body(n, unused):
            for j in range(9):
                k = n * 9 + j
                block = weight[pl.ds(pl.multiple_of((26 - k) * C, C), C), :].T
                out[pl.ds(pl.multiple_of(k * C, C), C), :] = block
            return unused

        lax.fori_loop(0, 3, body, 0)


def clear_band(wide):
    wide[27 * C : 36 * C, 0:C] = jnp.zeros((9 * C, C), BF16)
    wide[0 : 9 * C, C : 2 * C] = jnp.zeros((9 * C, C), BF16)


def pairs(gets, wide):
    parts, sizes = [], None
    for j in range(4):
        for b in range(3):
            pieces = [get(j, b) for get in gets]
            pieces = [piece.reshape(-1, piece.shape[-1]) for piece in pieces]
            sizes = [piece.shape[0] for piece in pieces]
            parts.append(pieces[0] if len(pieces) == 1 else jnp.concatenate(pieces, axis=0))
    value = jnp.dot(jnp.concatenate(parts, axis=1), wide[...], preferred_element_type=F32)
    results, at = [], 0
    for size in sizes:
        results.append((value[at : at + size, 0:C], value[at : at + size, C : 2 * C]))
        at += size
    return results


def rounded(value):
    return value.astype(BF16).astype(F32)


def slope_of(value):
    sig = jax.nn.sigmoid(value)
    return sig * (1.0 + value * (1.0 - sig))


def live_rows(tab):
    parts = [
        jnp.where(tab[OWN, s * 27 + 13] < ZERO, jnp.ones((BE, C), F32), jnp.zeros((BE, C), F32))
        for s in range(NB)
    ]
    return jnp.concatenate(parts, axis=0)


def zero_slot(field):
    def body(x, unused):
        field[x, :, ZERO : ZERO + BE, :] = jnp.zeros((field.shape[1], BE, C), F32)
        return unused

    lax.fori_loop(0, field.shape[0], body, 0)


def rows_at(field, x, y, value):
    n, m = value.shape[:2]
    field[x : x + n, y : y + m, 0:ROWS, :] = value


def weight_grad(patch, grads, turned, out, which, scale):
    for x in range(BE):
        block = grads[x].reshape(BE * ROWS, C).T
        for a in range(3):
            at = (x + a) * BE * ROWS
            turned[a * C : (a + 1) * C, at : at + BE * ROWS] = block

    right = jnp.concatenate([patch[:, b : b + BE].reshape((BE + 2) * BE * ROWS, 3 * C) for b in range(3)], axis=1)
    term = (jnp.dot(turned[...], right, preferred_element_type=F32) * scale).astype(BF16)
    for a in range(3):
        for j in range(9):
            at = (a * 9 + j) * C
            out[which, at : at + C, :] = term[a * C : (a + 1) * C, j * C : (j + 1) * C].T


def clear_turned(turned):
    width = BE * ROWS
    for a in range(3):
        for x in list(range(a)) + list(range(a + BE, BE + 2)):
            turned[a * C : (a + 1) * C, x * width : (x + 1) * width] = jnp.zeros((C, width), BF16)


def load_tables(lines, staged, tab, sem):
    for column, (ref, at) in lines.items():
        staged[column : column + 1, :] = ref[at, 0:16, :].astype(F32)[0:1].astype(jnp.int32)
    copy = pltpu.make_async_copy(staged, tab, sem)
    copy.start()
    copy.wait()


def first_payload_kernel(links, count, x_far, cot_far, xlow, xhigh, ylow, yhigh, own, x, cot, sems):
    copies = [pltpu.make_async_copy(x_far, x, sems.at[0]), pltpu.make_async_copy(cot_far, cot, sems.at[1])]
    for copy in copies:
        copy.start()
    lane = lax.broadcasted_iota(jnp.int32, (ROWS, C), 1)
    row = jnp.zeros((ROWS, C), jnp.int32)
    for s in range(NB):
        for d in range(27):
            if d == 13:
                named = jnp.where(s < count[0], s, -1)
            else:
                named = links[s, d if d < 13 else d - 1]
            start = jnp.where(named < 0, NB, named) * BE
            row = jnp.where(lane == s * 27 + d, start, row)
    line = row.astype(F32).astype(BF16)
    own[0] = line
    for copy in copies:
        copy.wait()
    for ref, xa, xc in ((xlow, 0, 0), (xhigh, 5, 7)):
        ref[0:24] = x[xa : xa + 3].reshape(24, ROWS, C)
        ref[24:32] = cot[xc]
        ref[32] = line
    for ref, ya, yc in ((ylow, 0, 0), (yhigh, 5, 7)):
        for i in range(BE):
            ref[3 * i : 3 * i + 3] = x[i, ya : ya + 3]
        ref[24:32] = cot[:, yc]
        ref[32] = line


def corner_payload_kernel(xm, xp, low, high):
    for ref, ya, yc in ((low, 0, 0), (high, 5, 7)):
        for j, near in enumerate((xm, xp)):
            for i in range(3):
                ref[9 * j + 3 * i : 9 * j + 3 * i + 3] = near[8 * i + ya : 8 * i + ya + 3]
            ref[18 + j] = near[24 + yc]
            ref[20 + j] = near[32]


def edge_payload_kernel(xm, xp, b1, low, high):
    for ref, y in ((low, 0), (high, 7)):
        ref[0] = xm[y]
        ref[1:9] = b1[:, y]
        ref[9] = xp[y]


def main_kernel(scale, core, *refs):
    far, own, refs = refs[:11], refs[11], refs[12:]
    out, b2o, b1o, elow, ehigh, gr = refs[:6]
    near, (sems, field, hid, back, p1, p2, px, py, pc, slope1, turned, wide, staged, tab, sem) = refs[6:17], refs[17:]
    x, cot, xm, xp, ym, yp, qm, qp, w1, w2, w2f = near
    copies = [pltpu.make_async_copy(far[i], near[i], sems.at[i]) for i in range(11)]
    order = [8, 0, 2, 3, 4, 5, 6, 7, 1, 9, 10]
    for i in order:
        copies[i].start()
    for ref in (field, hid, back):
        zero_slot(ref)
    clear_turned(turned)
    clear_band(wide)
    copies[8].wait()
    band(w1, wide)
    for i in order[1:8]:
        copies[i].wait()
    load_tables(
        {0: (qm, 20), 1: (xm, 32), 2: (qp, 20), 3: (ym, 32), 4: (own, 0), 5: (yp, 32), 6: (qm, 21), 7: (xp, 32), 8: (qp, 21)},
        staged, tab, sem,
    )
    live = live_rows(tab)

    def fill(i, unused):
        field[3 + i, 3:11, 0:ROWS, :] = x[i].astype(F32)
        field[3 + i, 0:3, 0:ROWS, :] = ym[pl.ds(3 * i, 3)].astype(F32)
        field[3 + i, 11:14, 0:ROWS, :] = yp[pl.ds(3 * i, 3)].astype(F32)
        return unused

    lax.fori_loop(0, BE, fill, 0)
    for i in range(3):
        for at, near, q in ((i, xm, 3 * i), (11 + i, xp, 9 + 3 * i)):
            field[at, 3:11, 0:ROWS, :] = near[8 * i : 8 * i + 8].astype(F32)
            field[at, 0:3, 0:ROWS, :] = qm[q : q + 3].astype(F32)
            field[at, 11:14, 0:ROWS, :] = qp[q : q + 3].astype(F32)

    ends = spans(2)
    corners = [0, 2, 6, 8]
    build_patches(tab, field, into(p1), 3, OWN, ends[0], ends[0])
    for j, cx in enumerate((-1, 1)):
        build_patches(tab, field, into(px, j), 3, COLUMNS.index((cx, 0)), ends[cx], ends[0])
        build_patches(tab, field, into(py, j), 3, COLUMNS.index((0, cx)), ends[0], ends[cx])
    for j, c in enumerate(corners):
        build_patches(tab, field, into(pc, j), 3, c, ends[COLUMNS[c][0]], ends[COLUMNS[c][1]])

    def hide(pre):
        return rounded(pre * jax.nn.sigmoid(pre))

    def own_pairs(patch, i):
        results = pairs([lambda j, b, g=g: patch[4 * i + g + j, b : b + BE] for g in (0, 2)], wide)
        return [(4 * i + 2 * g + h, results[g][h].reshape(BE, ROWS, C)) for g in range(2) for h in range(2)]

    def y_pairs(m):
        gets = [lambda j, b, s=s, p=p: py[s, 2 * p + j, b : b + m] for s in range(2) for p in range(4)]
        results = pairs(gets, wide)
        return [
            (s, 2 * p + h, results[4 * s + p][h].reshape(m, ROWS, C)) for s in range(2) for p in range(4) for h in range(2)
        ]

    def first_own(i, unused):
        for at, pre in own_pairs(p1, i):
            slope1[at] = slope_of(pre)
            hid[2 + at, 2:10, 0:ROWS, :] = hide(pre)
        return unused

    for i in range(2):
        first_own(i, 0)
    results = pairs([lambda j, b, s=s: px[s, j, b : b + BE] for s in range(2)], wide)
    for s in range(2):
        for h in range(2):
            hid[10 * s + h, 2:10, 0:ROWS, :] = hide(results[s][h]).reshape(BE, ROWS, C)
    for s, at, pre in y_pairs(2):
        hid[2 + at, 10 * s : 10 * s + 2, 0:ROWS, :] = hide(pre)
    [result] = pairs([lambda j, b: pc[:, j, b : b + 2]], wide)
    for h in range(2):
        value = hide(result[h]).reshape(4, 2, ROWS, C)
        for j, (ax, ay) in enumerate(((0, 0), (0, 10), (10, 0), (10, 10))):
            hid[ax + h, ay : ay + 2, 0:ROWS, :] = value[j]

    ends = spans(1)
    for i in order[8:]:
        copies[i].wait()
    band(w2, wide)
    build_patches(tab, hid, into(p2), 2, OWN, ends[0], ends[0])
    for j, cx in enumerate((-1, 1)):
        build_patches(tab, hid, into(px, j), 2, COLUMNS.index((cx, 0)), ends[cx], ends[0])
        build_patches(tab, hid, into(py, j), 2, COLUMNS.index((0, cx)), ends[0], ends[cx])
    for j, c in enumerate(corners):
        build_patches(tab, hid, into(pc, j), 2, c, ends[COLUMNS[c][0]], ends[COLUMNS[c][1]])

    def second_own(i, unused):
        for at, pre in own_pairs(p2, i):
            total = field[3 + at, 3:11, 0:ROWS, :] * live + pre
            sig = jax.nn.sigmoid(total)
            out[at] = (total * sig * live).astype(BF16)
            slope = sig * (1.0 + total * (1.0 - sig))
            grad = (cot[at].astype(F32) * slope * live).astype(BF16)
            b2o[at] = grad
            back[1 + at, 1:9, 0:ROWS, :] = grad.astype(F32)
        return unused

    for i in range(2):
        second_own(i, 0)
    for s, at, pre in y_pairs(1):
        near = (ym, yp)[s]
        total = field[3 + at, (2, 11)[s], 0:ROWS, :] + pre[0]
        back[1 + at, 9 * s, 0:ROWS, :] = rounded(near[24 + at].astype(F32) * slope_of(total))
    pre = product(lambda a, b: px[:, a : a + 1, b : b + BE], w2).reshape(2, BE, ROWS, C)
    for j, (at, cx, near) in enumerate(((2, 0, xm), (11, 9, xp))):
        total = field[at, 3:11, 0:ROWS, :] + pre[j]
        back[cx, 1:9, 0:ROWS, :] = rounded(near[24:32].astype(F32) * slope_of(total))
    pre = product(lambda a, b: pc[:, a : a + 1, b : b + 1], w2).reshape(4, ROWS, C)
    for j, (ax, ay, cx, cy, near, at) in enumerate(
        ((2, 2, 0, 0, qm, 18), (2, 11, 0, 9, qp, 18), (11, 2, 9, 0, qm, 19), (11, 11, 9, 9, qp, 19))
    ):
        total = field[ax, ay, 0:ROWS, :] + pre[j]
        back[cx, cy, 0:ROWS, :] = rounded(near[at].astype(F32) * slope_of(total))
    @pl.when(core[0] >= 0)
    def second_weight_grad():
        weight_grad(p2, b2o, turned, gr, 1 - core[0], scale)

    band(w2f, wide)
    build_patches(tab, back, into(p2), 1, OWN, (0, BE), (0, BE))

    def third(i, unused):
        for at, pre in own_pairs(p2, i):
            b1o[at] = (pre * slope1[at] * live).astype(BF16)
        return unused

    for i in range(2):
        third(i, 0)
    elow[...] = b1o[0]
    ehigh[...] = b1o[7]
    @pl.when(core[0] >= 0)
    def first_weight_grad():
        weight_grad(p1, b1o, turned, gr, core[0], scale)


def last_kernel(own, b1, b2, xm, xp, ym, yp, w1f, out, field, patch, wide, staged, tab, sem):
    load_tables({OWN: (own, 0)}, staged, tab, sem)
    live = live_rows(tab)
    zero_slot(field)
    clear_band(wide)
    band(w1f, wide)

    def fill(i, unused):
        field[1 + i, 1:9, 0:ROWS, :] = b1[i].astype(F32)
        return unused

    lax.fori_loop(0, BE, fill, 0)
    field[0, 1:9, 0:ROWS, :] = xm[...].astype(F32)
    field[9, 1:9, 0:ROWS, :] = xp[...].astype(F32)
    field[:, 0, 0:ROWS, :] = ym[...].astype(F32)
    field[:, 9, 0:ROWS, :] = yp[...].astype(F32)
    build_patches(tab, field, into(patch), 1, OWN, (0, BE), (0, BE))

    def step(i, unused):
        results = pairs([lambda j, b, g=g: patch[4 * i + g + j, b : b + BE] for g in (0, 2)], wide)
        for g in range(2):
            for h in range(2):
                at = 4 * i + 2 * g + h
                out[at] = ((b2[at].astype(F32) + results[g][h].reshape(BE, ROWS, C)) * live).astype(BF16)
        return unused

    for i in range(2):
        step(i, 0)


def call(kernel, outs, scratch, cost, mib, scalars, far, *args):
    smem = pl.BlockSpec(memory_space=pltpu.SMEM)
    vmem = pl.BlockSpec(memory_space=pltpu.VMEM)
    anywhere = pl.BlockSpec(memory_space=pltpu.HBM)
    args = [
        pltpu.with_memory_space_constraint(arg, pltpu.HBM) if scalars <= i < scalars + far else arg
        for i, arg in enumerate(args)
    ]
    return pl.pallas_call(
        kernel,
        out_shape=outs,
        in_specs=[smem] * scalars + [anywhere] * far + [vmem] * (len(args) - scalars - far),
        out_specs=jax.tree.map(lambda o: vmem, outs),
        scratch_shapes=scratch,
        compiler_params=pltpu.CompilerParams(vmem_limit_bytes=mib * 2**20),
        cost_estimate=pl.CostEstimate(flops=cost[0], bytes_accessed=cost[1], transcendentals=0),
    )(*args)


def swap_cores(part):
    return lax.ppermute(part, "dp", [(0, 1), (1, 0)])


def sum_scatter(part, axis):
    n = lax.axis_size(axis)
    swapped = lax.all_to_all(part.reshape(n, part.shape[0] // n, C), axis, 0, 0, tiled=True)
    return jnp.sum(swapped.astype(F32), axis=0).astype(BF16)


def sum_pairs(part, axis):
    n = lax.axis_size(axis)
    reach = 1
    while reach < n:
        other = lax.ppermute(part, axis, [(i, i ^ (2 * reach - 1)) for i in range(n)])
        part = (part.astype(F32) + other.astype(F32)).astype(BF16)
        reach *= 2
    return part


def gather_axis(part, axis):
    n = lax.axis_size(axis)
    copies = jnp.broadcast_to(part[None], (n,) + part.shape)
    return lax.all_to_all(copies, axis, 0, 0, tiled=True).reshape(n * part.shape[0], C)


def shape_of(*sizes):
    return jax.ShapeDtypeStruct(sizes, BF16)


def shards(features, cotangent, first_weight, second_weight, neighbours, counts):
    x = features.reshape(BE, BE, ROWS, C)
    cot = cotangent.reshape(BE, BE, ROWS, C)
    w1, w2 = first_weight.reshape(27 * C, C), second_weight.reshape(27 * C, C)
    n_devices = lax.axis_size("sx") * lax.axis_size("sy") * lax.axis_size("dp")
    scale = float(n_devices * NB * BE**3) ** -0.5
    core = lax.axis_index("dp").astype(jnp.int32)

    payload = shape_of(33, ROWS, C)
    xlow, xhigh, ylow, yhigh, own = call(
        first_payload_kernel, [payload] * 4 + [shape_of(1, ROWS, C)],
        [pltpu.VMEM((BE, BE, ROWS, C), BF16)] * 2 + [pltpu.SemaphoreType.DMA((2,))], (0, 2**21), 8, 2, 2,
        neighbours.reshape(NB, 26), counts.reshape(1), x, cot,
    )
    xm, xp = shift_pair(xlow, xhigh, "sx")
    ym, yp = shift_pair(ylow, yhigh, "sy")
    qlow, qhigh = call(corner_payload_kernel, [shape_of(22, ROWS, C)] * 2, [], (0, 2**19), 8, 0, 0, xm, xp)
    held1, held2, qlow, qhigh = lax.optimization_barrier((w1, w2, qlow, qhigh))
    qm, qp = shift_pair(qlow, qhigh, "sy")
    w1f, w2f = call(flip_kernel, [shape_of(27 * C, C)] * 2, [], (2**24, 2**22), 8, 0, 0, held1, held2)

    block, edge = shape_of(BE, BE, ROWS, C), shape_of(BE, ROWS, C)
    lanes = 3 * C
    unit = 2 * BE * BE * ROWS * 27 * C * C
    tables = [pltpu.VMEM((16, C), jnp.int32), pltpu.SMEM((16, C), jnp.int32), pltpu.SemaphoreType.DMA]
    out, b2, b1, elow, ehigh, grads = call(
        functools.partial(main_kernel, scale),
        [block, block, block, edge, edge, shape_of(2, 27 * C, C)],
        [
            *[pltpu.VMEM((BE, BE, ROWS, C), BF16)] * 2,
            *[pltpu.VMEM((33, ROWS, C), BF16)] * 4,
            *[pltpu.VMEM((22, ROWS, C), BF16)] * 2,
            *[pltpu.VMEM((27 * C, C), BF16)] * 3,
            pltpu.SemaphoreType.DMA((11,)),
            pltpu.VMEM((14, 14, ROWS + BE, C), F32),
            pltpu.VMEM((12, 12, ROWS + BE, C), F32),
            pltpu.VMEM((10, 10, ROWS + BE, C), F32),
            pltpu.VMEM((10, 10, ROWS, lanes), BF16),
            pltpu.VMEM((10, 10, ROWS, lanes), BF16),
            pltpu.VMEM((2, 4, 10, ROWS, lanes), BF16),
            pltpu.VMEM((2, 10, 4, ROWS, lanes), BF16),
            pltpu.VMEM((4, 4, 4, ROWS, lanes), BF16),
            pltpu.VMEM((BE, BE, ROWS, C), F32),
            pltpu.VMEM((3 * C, (BE + 2) * BE * ROWS), BF16),
            pltpu.VMEM((36 * C, 2 * C), BF16),
            *tables,
        ],
        (7 * unit, 10 * 2**20), 40, 1, 11,
        core.reshape(1), x, cot, xm, xp, ym, yp, qm, qp, w1, w2, w2f, own,
    )

    received = swap_cores(grads[1])
    bxm, bxp = shift_pair(elow, ehigh, "sx")
    part = (grads[0].astype(F32) + received.astype(F32)).astype(BF16)
    part, bxm, bxp = lax.optimization_barrier((sum_scatter(part, "sy"), bxm, bxp))
    blow, bhigh = call(edge_payload_kernel, [shape_of(BE + 2, ROWS, C)] * 2, [], (0, 2**19), 8, 0, 0, bxm, bxp, b1)
    bym, byp = shift_pair(blow, bhigh, "sy")
    part, bym, byp, b2 = lax.optimization_barrier((sum_pairs(part, "sx"), bym, byp, b2))

    grad_input = call(
        last_kernel,
        block,
        [
            pltpu.VMEM((10, 10, ROWS + BE, C), F32),
            pltpu.VMEM((10, 10, ROWS, lanes), BF16),
            pltpu.VMEM((36 * C, 2 * C), BF16),
            *tables,
        ],
        (unit, 4 * 2**20), 12, 0, 0,
        own, b1, b2, bxm, bxp, bym, byp, w1f,
    )
    part, grad_input = lax.optimization_barrier((gather_axis(part, "sy"), grad_input))
    part = part.reshape(27, C, C)
    other = swap_cores(part)
    first = jnp.where(core == 0, part, other).astype(F32)
    second = jnp.where(core == 0, other, part).astype(F32)
    shape = features.shape
    return out.reshape(shape), grad_input.reshape(shape), first, second


def solution(mesh):
    column = P("dp", "sx", "sy", None, None, None)
    return jax.shard_map(
        shards,
        mesh=mesh,
        in_specs=(column, column, P(), P(), P("dp", "sx", "sy", None, None), P("dp", "sx", "sy")),
        out_specs=(column, column, P(), P()),
        check_vma=False,
    )
```

```python
import functools

import jax
import jax.numpy as jnp
from jax import lax
from jax.experimental import pallas as pl
from jax.experimental.pallas import tpu as pltpu
from jax.sharding import PartitionSpec as P

C = 128
BE = 8
NB = 4
ROWS = NB * BE
ZERO = ROWS
F32 = jnp.float32
BF16 = jnp.bfloat16
COLUMNS = [(cx, cy) for cx in (-1, 0, 1) for cy in (-1, 0, 1)]
OWN = 4


def shift_pair(low, high, axis):
    n = lax.axis_size(axis)
    from_low = lax.ppermute(high, axis, [(i, (i + 1) % n) for i in range(n)])
    from_high = lax.ppermute(low, axis, [((i + 1) % n, i) for i in range(n)])
    return from_low, from_high


def spans(halo):
    return {-1: (0, halo), 0: (halo, halo + BE), 1: (halo + BE, 2 * halo + BE)}


def build_patches(tab, field, put, halo, column, xs, ys):
    cx, cy = COLUMNS[column]
    row = lax.broadcasted_iota(jnp.int32, (1, BE, C), 1)
    for sx, (x0, x1) in spans(halo).items():
        xa, xb = max(x0, xs[0]), min(x1, xs[1] + 2)
        if xa >= xb:
            continue
        for sy, (y0, y1) in spans(halo).items():
            ya, yb = max(y0, ys[0]), min(y1, ys[1] + 2)
            if ya >= yb:
                continue
            first = (sx - cx + 1) * 9 + (sy - cy + 1) * 3
            offsets = [
                [pl.multiple_of(tab[column, s * 27 + first + j], BE) for j in range(3)]
                for s in range(NB)
            ]

            def line(x):
                parts = [[], [], []]
                for below, here, above in offsets:
                    v = field[x, ya:yb, pl.ds(here, BE), :]
                    lo = field[x, ya:yb, pl.ds(below, BE), :]
                    hi = field[x, ya:yb, pl.ds(above, BE), :]
                    parts[0].append(pltpu.roll(jnp.where(row == BE - 1, lo, v), 1, 1))
                    parts[1].append(v)
                    parts[2].append(pltpu.roll(jnp.where(row == 0, hi, v), BE - 1, 1))
                for j in range(3):
                    value = jnp.concatenate(parts[j], axis=1).astype(BF16)
                    put(x - xs[0], ya - ys[0], yb - ys[0], j * C, value)

            if xb - xa > 8:

                def body(x, unused):
                    line(x)
                    return unused

                lax.fori_loop(xa, xb, body, 0)
            else:
                for x in range(xa, xb):
                    line(x)


def into(ref, lead=None):
    def put(x, ya, yb, lane, value):
        if lead is None:
            ref[x, ya:yb, :, lane : lane + C] = value
        else:
            ref[lead, x, ya:yb, :, lane : lane + C] = value

    return put


def product(get, weight):
    parts = []
    for a in range(3):
        for b in range(3):
            piece = get(a, b)
            parts.append(piece.reshape(-1, piece.shape[-1]))
    return jnp.dot(jnp.concatenate(parts, axis=1), weight[...], preferred_element_type=F32)


def band(weight, wide):
    wide[0 : 27 * C, 0:C] = weight[...]
    wide[9 * C : 36 * C, C : 2 * C] = weight[...]


def flip(weight, out):
    for k in range(27):
        out[k * C : (k + 1) * C, :] = weight[(26 - k) * C : (27 - k) * C, :].T


def clear_band(wide):
    wide[27 * C : 36 * C, 0:C] = jnp.zeros((9 * C, C), BF16)
    wide[0 : 9 * C, C : 2 * C] = jnp.zeros((9 * C, C), BF16)


def pairs(gets, wide):
    parts, sizes = [], None
    for j in range(4):
        for b in range(3):
            pieces = [get(j, b) for get in gets]
            pieces = [piece.reshape(-1, piece.shape[-1]) for piece in pieces]
            sizes = [piece.shape[0] for piece in pieces]
            parts.append(pieces[0] if len(pieces) == 1 else jnp.concatenate(pieces, axis=0))
    value = jnp.dot(jnp.concatenate(parts, axis=1), wide[...], preferred_element_type=F32)
    results, at = [], 0
    for size in sizes:
        results.append((value[at : at + size, 0:C], value[at : at + size, C : 2 * C]))
        at += size
    return results


def rounded(value):
    return value.astype(BF16).astype(F32)


def slope_of(value):
    sig = jax.nn.sigmoid(value)
    return sig * (1.0 + value * (1.0 - sig))


def live_rows(tab):
    parts = [
        jnp.where(tab[OWN, s * 27 + 13] < ZERO, jnp.ones((BE, C), F32), jnp.zeros((BE, C), F32))
        for s in range(NB)
    ]
    return jnp.concatenate(parts, axis=0)


def zero_slot(field):
    def body(x, unused):
        field[x, :, ZERO : ZERO + BE, :] = jnp.zeros((field.shape[1], BE, C), F32)
        return unused

    lax.fori_loop(0, field.shape[0], body, 0)


def rows_at(field, x, y, value):
    n, m = value.shape[:2]
    field[x : x + n, y : y + m, 0:ROWS, :] = value


def weight_grad(patch, grads, turned, out, which, scale):
    for x in range(BE):
        block = grads[x].reshape(BE * ROWS, C).T
        for a in range(3):
            at = (x + a) * BE * ROWS
            turned[a * C : (a + 1) * C, at : at + BE * ROWS] = block

    right = jnp.concatenate([patch[:, b : b + BE].reshape((BE + 2) * BE * ROWS, 3 * C) for b in range(3)], axis=1)
    term = (jnp.dot(turned[...], right, preferred_element_type=F32) * scale).astype(BF16)
    for a in range(3):
        for j in range(9):
            at = (a * 9 + j) * C
            out[which, at : at + C, :] = term[a * C : (a + 1) * C, j * C : (j + 1) * C].T


def clear_turned(turned):
    width = BE * ROWS
    for a in range(3):
        for x in list(range(a)) + list(range(a + BE, BE + 2)):
            turned[a * C : (a + 1) * C, x * width : (x + 1) * width] = jnp.zeros((C, width), BF16)


def load_tables(lines, staged, tab, sem):
    for column, (ref, at) in lines.items():
        staged[column : column + 1, :] = ref[at, 0:16, :].astype(F32)[0:1].astype(jnp.int32)
    copy = pltpu.make_async_copy(staged, tab, sem)
    copy.start()
    copy.wait()


def first_payload_kernel(links, count, x_far, cot_far, xlow, xhigh, ylow, yhigh, own, x, cot, sems):
    copies = [pltpu.make_async_copy(x_far, x, sems.at[0]), pltpu.make_async_copy(cot_far, cot, sems.at[1])]
    for copy in copies:
        copy.start()
    lane = lax.broadcasted_iota(jnp.int32, (ROWS, C), 1)
    row = jnp.zeros((ROWS, C), jnp.int32)
    for s in range(NB):
        for d in range(27):
            if d == 13:
                named = jnp.where(s < count[0], s, -1)
            else:
                named = links[s, d if d < 13 else d - 1]
            start = jnp.where(named < 0, NB, named) * BE
            row = jnp.where(lane == s * 27 + d, start, row)
    line = row.astype(F32).astype(BF16)
    own[0] = line
    for copy in copies:
        copy.wait()
    for ref, xa, xc in ((xlow, 0, 0), (xhigh, 5, 7)):
        ref[0:24] = x[xa : xa + 3].reshape(24, ROWS, C)
        ref[24:32] = cot[xc]
        ref[32] = line
    for ref, ya, yc in ((ylow, 0, 0), (yhigh, 5, 7)):
        for i in range(BE):
            ref[3 * i : 3 * i + 3] = x[i, ya : ya + 3]
        ref[24:32] = cot[:, yc]
        ref[32] = line


def corner_payload_kernel(xm, xp, low, high):
    for ref, ya, yc in ((low, 0, 0), (high, 5, 7)):
        for j, near in enumerate((xm, xp)):
            for i in range(3):
                ref[9 * j + 3 * i : 9 * j + 3 * i + 3] = near[8 * i + ya : 8 * i + ya + 3]
            ref[18 + j] = near[24 + yc]
            ref[20 + j] = near[32]


def edge_payload_kernel(xm, xp, b1, low, high):
    for ref, y in ((low, 0), (high, 7)):
        ref[0] = xm[y]
        ref[1:9] = b1[:, y]
        ref[9] = xp[y]


def main_kernel(scale, core, *refs):
    far, own, refs = refs[:10], refs[10], refs[11:]
    out, b2o, b1o, elow, ehigh, gr = refs[:6]
    near, (w2f, sems, field, hid, back, p1, p2, px, py, pc, slope1, turned, wide, staged, tab, sem) = refs[6:16], refs[16:]
    x, cot, xm, xp, ym, yp, qm, qp, w1, w2 = near
    copies = [pltpu.make_async_copy(far[i], near[i], sems.at[i]) for i in range(10)]
    order = [8, 0, 2, 3, 4, 5, 6, 7, 9, 1]
    for i in order:
        copies[i].start()
    for ref in (field, hid, back):
        zero_slot(ref)
    clear_turned(turned)
    clear_band(wide)
    copies[8].wait()
    band(w1, wide)
    for i in order[1:]:
        copies[i].wait()
    load_tables(
        {0: (qm, 20), 1: (xm, 32), 2: (qp, 20), 3: (ym, 32), 4: (own, 0), 5: (yp, 32), 6: (qm, 21), 7: (xp, 32), 8: (qp, 21)},
        staged, tab, sem,
    )
    live = live_rows(tab)

    def fill(i, unused):
        field[3 + i, 3:11, 0:ROWS, :] = x[i].astype(F32)
        field[3 + i, 0:3, 0:ROWS, :] = ym[pl.ds(3 * i, 3)].astype(F32)
        field[3 + i, 11:14, 0:ROWS, :] = yp[pl.ds(3 * i, 3)].astype(F32)
        return unused

    lax.fori_loop(0, BE, fill, 0)
    for i in range(3):
        for at, near, q in ((i, xm, 3 * i), (11 + i, xp, 9 + 3 * i)):
            field[at, 3:11, 0:ROWS, :] = near[8 * i : 8 * i + 8].astype(F32)
            field[at, 0:3, 0:ROWS, :] = qm[q : q + 3].astype(F32)
            field[at, 11:14, 0:ROWS, :] = qp[q : q + 3].astype(F32)

    ends = spans(2)
    corners = [0, 2, 6, 8]
    build_patches(tab, field, into(p1), 3, OWN, ends[0], ends[0])
    for j, cx in enumerate((-1, 1)):
        build_patches(tab, field, into(px, j), 3, COLUMNS.index((cx, 0)), ends[cx], ends[0])
        build_patches(tab, field, into(py, j), 3, COLUMNS.index((0, cx)), ends[0], ends[cx])
    for j, c in enumerate(corners):
        build_patches(tab, field, into(pc, j), 3, c, ends[COLUMNS[c][0]], ends[COLUMNS[c][1]])

    flip(w2, w2f)

    def hide(pre):
        return rounded(pre * jax.nn.sigmoid(pre))

    def own_pairs(patch, i):
        results = pairs([lambda j, b, g=g: patch[4 * i + g + j, b : b + BE] for g in (0, 2)], wide)
        return [(4 * i + 2 * g + h, results[g][h].reshape(BE, ROWS, C)) for g in range(2) for h in range(2)]

    def y_pairs(m):
        gets = [lambda j, b, s=s, p=p: py[s, 2 * p + j, b : b + m] for s in range(2) for p in range(4)]
        results = pairs(gets, wide)
        return [
            (s, 2 * p + h, results[4 * s + p][h].reshape(m, ROWS, C)) for s in range(2) for p in range(4) for h in range(2)
        ]

    def first_own(i, unused):
        for at, pre in own_pairs(p1, i):
            slope1[at] = slope_of(pre)
            hid[2 + at, 2:10, 0:ROWS, :] = hide(pre)
        return unused

    for i in range(2):
        first_own(i, 0)
    results = pairs([lambda j, b, s=s: px[s, j, b : b + BE] for s in range(2)], wide)
    for s in range(2):
        for h in range(2):
            hid[10 * s + h, 2:10, 0:ROWS, :] = hide(results[s][h]).reshape(BE, ROWS, C)
    for s, at, pre in y_pairs(2):
        hid[2 + at, 10 * s : 10 * s + 2, 0:ROWS, :] = hide(pre)
    [result] = pairs([lambda j, b: pc[:, j, b : b + 2]], wide)
    for h in range(2):
        value = hide(result[h]).reshape(4, 2, ROWS, C)
        for j, (ax, ay) in enumerate(((0, 0), (0, 10), (10, 0), (10, 10))):
            hid[ax + h, ay : ay + 2, 0:ROWS, :] = value[j]

    ends = spans(1)
    band(w2, wide)
    build_patches(tab, hid, into(p2), 2, OWN, ends[0], ends[0])
    for j, cx in enumerate((-1, 1)):
        build_patches(tab, hid, into(px, j), 2, COLUMNS.index((cx, 0)), ends[cx], ends[0])
        build_patches(tab, hid, into(py, j), 2, COLUMNS.index((0, cx)), ends[0], ends[cx])
    for j, c in enumerate(corners):
        build_patches(tab, hid, into(pc, j), 2, c, ends[COLUMNS[c][0]], ends[COLUMNS[c][1]])

    def second_own(i, unused):
        for at, pre in own_pairs(p2, i):
            total = field[3 + at, 3:11, 0:ROWS, :] * live + pre
            sig = jax.nn.sigmoid(total)
            out[at] = (total * sig * live).astype(BF16)
            slope = sig * (1.0 + total * (1.0 - sig))
            grad = (cot[at].astype(F32) * slope * live).astype(BF16)
            b2o[at] = grad
            back[1 + at, 1:9, 0:ROWS, :] = grad.astype(F32)
        return unused

    for i in range(2):
        second_own(i, 0)
    for s, at, pre in y_pairs(1):
        near = (ym, yp)[s]
        total = field[3 + at, (2, 11)[s], 0:ROWS, :] + pre[0]
        back[1 + at, 9 * s, 0:ROWS, :] = rounded(near[24 + at].astype(F32) * slope_of(total))
    pre = product(lambda a, b: px[:, a : a + 1, b : b + BE], w2).reshape(2, BE, ROWS, C)
    for j, (at, cx, near) in enumerate(((2, 0, xm), (11, 9, xp))):
        total = field[at, 3:11, 0:ROWS, :] + pre[j]
        back[cx, 1:9, 0:ROWS, :] = rounded(near[24:32].astype(F32) * slope_of(total))
    pre = product(lambda a, b: pc[:, a : a + 1, b : b + 1], w2).reshape(4, ROWS, C)
    for j, (ax, ay, cx, cy, near, at) in enumerate(
        ((2, 2, 0, 0, qm, 18), (2, 11, 0, 9, qp, 18), (11, 2, 9, 0, qm, 19), (11, 11, 9, 9, qp, 19))
    ):
        total = field[ax, ay, 0:ROWS, :] + pre[j]
        back[cx, cy, 0:ROWS, :] = rounded(near[at].astype(F32) * slope_of(total))
    @pl.when(core[0] >= 0)
    def second_weight_grad():
        weight_grad(p2, b2o, turned, gr, 1 - core[0], scale)

    band(w2f, wide)
    build_patches(tab, back, into(p2), 1, OWN, (0, BE), (0, BE))

    def third(i, unused):
        for at, pre in own_pairs(p2, i):
            b1o[at] = (pre * slope1[at] * live).astype(BF16)
        return unused

    for i in range(2):
        third(i, 0)
    elow[...] = b1o[0]
    ehigh[...] = b1o[7]
    @pl.when(core[0] >= 0)
    def first_weight_grad():
        weight_grad(p1, b1o, turned, gr, core[0], scale)


def last_kernel(own, b1, b2, xm, xp, ym, yp, w1, out, field, patch, w1f, wide, staged, tab, sem):
    load_tables({OWN: (own, 0)}, staged, tab, sem)
    live = live_rows(tab)
    zero_slot(field)
    clear_band(wide)
    flip(w1, w1f)
    band(w1f, wide)

    def fill(i, unused):
        field[1 + i, 1:9, 0:ROWS, :] = b1[i].astype(F32)
        return unused

    lax.fori_loop(0, BE, fill, 0)
    field[0, 1:9, 0:ROWS, :] = xm[...].astype(F32)
    field[9, 1:9, 0:ROWS, :] = xp[...].astype(F32)
    field[:, 0, 0:ROWS, :] = ym[...].astype(F32)
    field[:, 9, 0:ROWS, :] = yp[...].astype(F32)
    build_patches(tab, field, into(patch), 1, OWN, (0, BE), (0, BE))

    def step(i, unused):
        results = pairs([lambda j, b, g=g: patch[4 * i + g + j, b : b + BE] for g in (0, 2)], wide)
        for g in range(2):
            for h in range(2):
                at = 4 * i + 2 * g + h
                out[at] = ((b2[at].astype(F32) + results[g][h].reshape(BE, ROWS, C)) * live).astype(BF16)
        return unused

    for i in range(2):
        step(i, 0)


def call(kernel, outs, scratch, cost, mib, scalars, far, *args):
    smem = pl.BlockSpec(memory_space=pltpu.SMEM)
    vmem = pl.BlockSpec(memory_space=pltpu.VMEM)
    anywhere = pl.BlockSpec(memory_space=pltpu.HBM)
    args = [
        pltpu.with_memory_space_constraint(arg, pltpu.HBM) if scalars <= i < scalars + far else arg
        for i, arg in enumerate(args)
    ]
    return pl.pallas_call(
        kernel,
        out_shape=outs,
        in_specs=[smem] * scalars + [anywhere] * far + [vmem] * (len(args) - scalars - far),
        out_specs=jax.tree.map(lambda o: vmem, outs),
        scratch_shapes=scratch,
        compiler_params=pltpu.CompilerParams(vmem_limit_bytes=mib * 2**20),
        cost_estimate=pl.CostEstimate(flops=cost[0], bytes_accessed=cost[1], transcendentals=0),
    )(*args)


def swap_cores(part):
    return lax.ppermute(part, "dp", [(0, 1), (1, 0)])


def sum_scatter(part, axis):
    n = lax.axis_size(axis)
    swapped = lax.all_to_all(part.reshape(n, part.shape[0] // n, C), axis, 0, 0, tiled=True)
    return jnp.sum(swapped.astype(F32), axis=0).astype(BF16)


def sum_pairs(part, axis):
    n = lax.axis_size(axis)
    reach = 1
    while reach < n:
        other = lax.ppermute(part, axis, [(i, i ^ (2 * reach - 1)) for i in range(n)])
        part = (part.astype(F32) + other.astype(F32)).astype(BF16)
        reach *= 2
    return part


def gather_axis(part, axis):
    n = lax.axis_size(axis)
    copies = jnp.broadcast_to(part[None], (n,) + part.shape)
    return lax.all_to_all(copies, axis, 0, 0, tiled=True).reshape(n * part.shape[0], C)


def shape_of(*sizes):
    return jax.ShapeDtypeStruct(sizes, BF16)


def shards(features, cotangent, first_weight, second_weight, neighbours, counts):
    x = features.reshape(BE, BE, ROWS, C)
    cot = cotangent.reshape(BE, BE, ROWS, C)
    w1, w2 = first_weight.reshape(27 * C, C), second_weight.reshape(27 * C, C)
    n_devices = lax.axis_size("sx") * lax.axis_size("sy") * lax.axis_size("dp")
    scale = float(n_devices * NB * BE**3) ** -0.5
    core = lax.axis_index("dp").astype(jnp.int32)

    payload = shape_of(33, ROWS, C)
    xlow, xhigh, ylow, yhigh, own = call(
        first_payload_kernel, [payload] * 4 + [shape_of(1, ROWS, C)],
        [pltpu.VMEM((BE, BE, ROWS, C), BF16)] * 2 + [pltpu.SemaphoreType.DMA((2,))], (0, 2**21), 8, 2, 2,
        neighbours.reshape(NB, 26), counts.reshape(1), x, cot,
    )
    xm, xp = shift_pair(xlow, xhigh, "sx")
    ym, yp = shift_pair(ylow, yhigh, "sy")
    qlow, qhigh = call(corner_payload_kernel, [shape_of(22, ROWS, C)] * 2, [], (0, 2**19), 8, 0, 0, xm, xp)
    qm, qp = shift_pair(qlow, qhigh, "sy")

    block, edge = shape_of(BE, BE, ROWS, C), shape_of(BE, ROWS, C)
    lanes = 3 * C
    unit = 2 * BE * BE * ROWS * 27 * C * C
    tables = [pltpu.VMEM((16, C), jnp.int32), pltpu.SMEM((16, C), jnp.int32), pltpu.SemaphoreType.DMA]
    out, b2, b1, elow, ehigh, grads = call(
        functools.partial(main_kernel, scale),
        [block, block, block, edge, edge, shape_of(2, 27 * C, C)],
        [
            *[pltpu.VMEM((BE, BE, ROWS, C), BF16)] * 2,
            *[pltpu.VMEM((33, ROWS, C), BF16)] * 4,
            *[pltpu.VMEM((22, ROWS, C), BF16)] * 2,
            *[pltpu.VMEM((27 * C, C), BF16)] * 3,
            pltpu.SemaphoreType.DMA((10,)),
            pltpu.VMEM((14, 14, ROWS + BE, C), F32),
            pltpu.VMEM((12, 12, ROWS + BE, C), F32),
            pltpu.VMEM((10, 10, ROWS + BE, C), F32),
            pltpu.VMEM((10, 10, ROWS, lanes), BF16),
            pltpu.VMEM((10, 10, ROWS, lanes), BF16),
            pltpu.VMEM((2, 4, 10, ROWS, lanes), BF16),
            pltpu.VMEM((2, 10, 4, ROWS, lanes), BF16),
            pltpu.VMEM((4, 4, 4, ROWS, lanes), BF16),
            pltpu.VMEM((BE, BE, ROWS, C), F32),
            pltpu.VMEM((3 * C, (BE + 2) * BE * ROWS), BF16),
            pltpu.VMEM((36 * C, 2 * C), BF16),
            *tables,
        ],
        (7 * unit, 10 * 2**20), 40, 1, 10,
        core.reshape(1), x, cot, xm, xp, ym, yp, qm, qp, w1, w2, own,
    )

    received = swap_cores(grads[1])
    bxm, bxp = shift_pair(elow, ehigh, "sx")
    part = (grads[0].astype(F32) + received.astype(F32)).astype(BF16)
    part, bxm, bxp = lax.optimization_barrier((sum_scatter(part, "sy"), bxm, bxp))
    blow, bhigh = call(edge_payload_kernel, [shape_of(BE + 2, ROWS, C)] * 2, [], (0, 2**19), 8, 0, 0, bxm, bxp, b1)
    bym, byp = shift_pair(blow, bhigh, "sy")
    part, bym, byp, b2 = lax.optimization_barrier((sum_pairs(part, "sx"), bym, byp, b2))

    grad_input = call(
        last_kernel,
        block,
        [
            pltpu.VMEM((10, 10, ROWS + BE, C), F32),
            pltpu.VMEM((10, 10, ROWS, lanes), BF16),
            pltpu.VMEM((27 * C, C), BF16),
            pltpu.VMEM((36 * C, 2 * C), BF16),
            *tables,
        ],
        (unit, 4 * 2**20), 12, 0, 0,
        own, b1, b2, bxm, bxp, bym, byp, w1,
    )
    part, grad_input = lax.optimization_barrier((gather_axis(part, "sy"), grad_input))
    part = part.reshape(27, C, C)
    other = swap_cores(part)
    first = jnp.where(core == 0, part, other).astype(F32)
    second = jnp.where(core == 0, other, part).astype(F32)
    shape = features.shape
    return out.reshape(shape), grad_input.reshape(shape), first, second


def solution(mesh):
    column = P("dp", "sx", "sy", None, None, None)
    return jax.shard_map(
        shards,
        mesh=mesh,
        in_specs=(column, column, P(), P(), P("dp", "sx", "sy", None, None), P("dp", "sx", "sy")),
        out_specs=(column, column, P(), P()),
        check_vma=False,
    )
```

```python
import functools

import jax
import jax.numpy as jnp
from jax import lax
from jax.experimental import pallas as pl
from jax.experimental.pallas import tpu as pltpu
from jax.sharding import PartitionSpec as P

C = 128
BE = 8
NB = 4
ROWS = NB * BE
ZERO = ROWS
F32 = jnp.float32
BF16 = jnp.bfloat16
COLUMNS = [(cx, cy) for cx in (-1, 0, 1) for cy in (-1, 0, 1)]
OWN = 4


def shift_pair(low, high, axis):
    n = lax.axis_size(axis)
    from_low = lax.ppermute(high, axis, [(i, (i + 1) % n) for i in range(n)])
    from_high = lax.ppermute(low, axis, [((i + 1) % n, i) for i in range(n)])
    return from_low, from_high


def spans(halo):
    return {-1: (0, halo), 0: (halo, halo + BE), 1: (halo + BE, 2 * halo + BE)}


def build_patches(tab, field, put, halo, column, xs, ys):
    cx, cy = COLUMNS[column]
    row = lax.broadcasted_iota(jnp.int32, (1, BE, C), 1)
    for sx, (x0, x1) in spans(halo).items():
        xa, xb = max(x0, xs[0]), min(x1, xs[1] + 2)
        if xa >= xb:
            continue
        for sy, (y0, y1) in spans(halo).items():
            ya, yb = max(y0, ys[0]), min(y1, ys[1] + 2)
            if ya >= yb:
                continue
            first = (sx - cx + 1) * 9 + (sy - cy + 1) * 3
            offsets = [
                [pl.multiple_of(tab[column, s * 27 + first + j], BE) for j in range(3)]
                for s in range(NB)
            ]

            def line(x):
                parts = [[], [], []]
                for below, here, above in offsets:
                    v = field[x, ya:yb, pl.ds(here, BE), :]
                    lo = field[x, ya:yb, pl.ds(below, BE), :]
                    hi = field[x, ya:yb, pl.ds(above, BE), :]
                    parts[0].append(pltpu.roll(jnp.where(row == BE - 1, lo, v), 1, 1))
                    parts[1].append(v)
                    parts[2].append(pltpu.roll(jnp.where(row == 0, hi, v), BE - 1, 1))
                for j in range(3):
                    value = jnp.concatenate(parts[j], axis=1).astype(BF16)
                    put(x - xs[0], ya - ys[0], yb - ys[0], j * C, value)

            if xb - xa > 8:

                def body(x, unused):
                    line(x)
                    return unused

                lax.fori_loop(xa, xb, body, 0)
            else:
                for x in range(xa, xb):
                    line(x)


def into(ref, lead=None):
    def put(x, ya, yb, lane, value):
        if lead is None:
            ref[x, ya:yb, :, lane : lane + C] = value
        else:
            ref[lead, x, ya:yb, :, lane : lane + C] = value

    return put


def product(get, weight):
    parts = []
    for a in range(3):
        for b in range(3):
            piece = get(a, b)
            parts.append(piece.reshape(-1, piece.shape[-1]))
    return jnp.dot(jnp.concatenate(parts, axis=1), weight[...], preferred_element_type=F32)


def band(weight, wide):
    wide[0 : 27 * C, 0:C] = weight[...]
    wide[9 * C : 36 * C, C : 2 * C] = weight[...]


def flip(weight, out):
    for k in range(27):
        out[k * C : (k + 1) * C, :] = weight[(26 - k) * C : (27 - k) * C, :].T


def clear_band(wide):
    wide[27 * C : 36 * C, 0:C] = jnp.zeros((9 * C, C), BF16)
    wide[0 : 9 * C, C : 2 * C] = jnp.zeros((9 * C, C), BF16)


def pairs(gets, wide):
    parts, sizes = [], None
    for j in range(4):
        for b in range(3):
            pieces = [get(j, b) for get in gets]
            pieces = [piece.reshape(-1, piece.shape[-1]) for piece in pieces]
            sizes = [piece.shape[0] for piece in pieces]
            parts.append(pieces[0] if len(pieces) == 1 else jnp.concatenate(pieces, axis=0))
    value = jnp.dot(jnp.concatenate(parts, axis=1), wide[...], preferred_element_type=F32)
    results, at = [], 0
    for size in sizes:
        results.append((value[at : at + size, 0:C], value[at : at + size, C : 2 * C]))
        at += size
    return results


def rounded(value):
    return value.astype(BF16).astype(F32)


def slope_of(value):
    sig = jax.nn.sigmoid(value)
    return sig * (1.0 + value * (1.0 - sig))


def live_rows(tab):
    parts = [
        jnp.where(tab[OWN, s * 27 + 13] < ZERO, jnp.ones((BE, C), F32), jnp.zeros((BE, C), F32))
        for s in range(NB)
    ]
    return jnp.concatenate(parts, axis=0)


def zero_slot(field):
    def body(x, unused):
        field[x, :, ZERO : ZERO + BE, :] = jnp.zeros((field.shape[1], BE, C), F32)
        return unused

    lax.fori_loop(0, field.shape[0], body, 0)


def rows_at(field, x, y, value):
    n, m = value.shape[:2]
    field[x : x + n, y : y + m, 0:ROWS, :] = value


def weight_grad(patch, grads, turned, out, which, scale):
    for x in range(BE):
        block = grads[x].reshape(BE * ROWS, C).T
        for a in range(3):
            at = (x + a) * BE * ROWS
            turned[a * C : (a + 1) * C, at : at + BE * ROWS] = block

    right = jnp.concatenate([patch[:, b : b + BE].reshape((BE + 2) * BE * ROWS, 3 * C) for b in range(3)], axis=1)
    term = (jnp.dot(turned[...], right, preferred_element_type=F32) * scale).astype(BF16)
    for a in range(3):
        for j in range(9):
            at = (a * 9 + j) * C
            out[which, at : at + C, :] = term[a * C : (a + 1) * C, j * C : (j + 1) * C].T


def clear_turned(turned):
    width = BE * ROWS
    for a in range(3):
        for x in list(range(a)) + list(range(a + BE, BE + 2)):
            turned[a * C : (a + 1) * C, x * width : (x + 1) * width] = jnp.zeros((C, width), BF16)


def load_tables(lines, staged, tab, sem):
    for column, (ref, at) in lines.items():
        staged[column : column + 1, :] = ref[at, 0:16, :].astype(F32)[0:1].astype(jnp.int32)
    copy = pltpu.make_async_copy(staged, tab, sem)
    copy.start()
    copy.wait()


def first_payload_kernel(links, count, x_far, cot_far, xlow, xhigh, ylow, yhigh, own, x, cot, sems):
    copies = [pltpu.make_async_copy(x_far, x, sems.at[0]), pltpu.make_async_copy(cot_far, cot, sems.at[1])]
    for copy in copies:
        copy.start()
    lane = lax.broadcasted_iota(jnp.int32, (ROWS, C), 1)
    row = jnp.zeros((ROWS, C), jnp.int32)
    for s in range(NB):
        for d in range(27):
            if d == 13:
                named = jnp.where(s < count[0], s, -1)
            else:
                named = links[s, d if d < 13 else d - 1]
            start = jnp.where(named < 0, NB, named) * BE
            row = jnp.where(lane == s * 27 + d, start, row)
    line = row.astype(F32).astype(BF16)
    own[0] = line
    for copy in copies:
        copy.wait()
    for ref, xa, xc in ((xlow, 0, 0), (xhigh, 5, 7)):
        ref[0:24] = x[xa : xa + 3].reshape(24, ROWS, C)
        ref[24:32] = cot[xc]
        ref[32] = line
    for ref, ya, yc in ((ylow, 0, 0), (yhigh, 5, 7)):
        for i in range(BE):
            ref[3 * i : 3 * i + 3] = x[i, ya : ya + 3]
        ref[24:32] = cot[:, yc]
        ref[32] = line


def corner_payload_kernel(xm, xp, low, high):
    for ref, ya, yc in ((low, 0, 0), (high, 5, 7)):
        for j, near in enumerate((xm, xp)):
            for i in range(3):
                ref[9 * j + 3 * i : 9 * j + 3 * i + 3] = near[8 * i + ya : 8 * i + ya + 3]
            ref[18 + j] = near[24 + yc]
            ref[20 + j] = near[32]


def edge_payload_kernel(xm, xp, b1, low, high):
    for ref, y in ((low, 0), (high, 7)):
        ref[0] = xm[y]
        ref[1:9] = b1[:, y]
        ref[9] = xp[y]


def main_kernel(scale, core, *refs):
    far, (xm, xp, ym, yp, qm, qp, own), refs = refs[:4], refs[4:11], refs[11:]
    out, b2o, b1o, elow, ehigh, gr = refs[:6]
    near, (w2f, sems, field, hid, back, p1, p2, px, py, pc, slope1, turned, wide, staged, tab, sem) = refs[6:10], refs[10:]
    x, cot, w1, w2 = near
    copies = [pltpu.make_async_copy(far[i], near[i], sems.at[i]) for i in range(4)]
    order = [2, 0, 3, 1]
    for i in order:
        copies[i].start()
    for ref in (field, hid, back):
        zero_slot(ref)
    clear_turned(turned)
    clear_band(wide)
    copies[2].wait()
    band(w1, wide)
    for i in order[1:]:
        copies[i].wait()
    load_tables(
        {0: (qm, 20), 1: (xm, 32), 2: (qp, 20), 3: (ym, 32), 4: (own, 0), 5: (yp, 32), 6: (qm, 21), 7: (xp, 32), 8: (qp, 21)},
        staged, tab, sem,
    )
    live = live_rows(tab)

    def fill(i, unused):
        field[3 + i, 3:11, 0:ROWS, :] = x[i].astype(F32)
        field[3 + i, 0:3, 0:ROWS, :] = ym[pl.ds(3 * i, 3)].astype(F32)
        field[3 + i, 11:14, 0:ROWS, :] = yp[pl.ds(3 * i, 3)].astype(F32)
        return unused

    lax.fori_loop(0, BE, fill, 0)
    for i in range(3):
        for at, near, q in ((i, xm, 3 * i), (11 + i, xp, 9 + 3 * i)):
            field[at, 3:11, 0:ROWS, :] = near[8 * i : 8 * i + 8].astype(F32)
            field[at, 0:3, 0:ROWS, :] = qm[q : q + 3].astype(F32)
            field[at, 11:14, 0:ROWS, :] = qp[q : q + 3].astype(F32)

    ends = spans(2)
    corners = [0, 2, 6, 8]
    build_patches(tab, field, into(p1), 3, OWN, ends[0], ends[0])
    for j, cx in enumerate((-1, 1)):
        build_patches(tab, field, into(px, j), 3, COLUMNS.index((cx, 0)), ends[cx], ends[0])
        build_patches(tab, field, into(py, j), 3, COLUMNS.index((0, cx)), ends[0], ends[cx])
    for j, c in enumerate(corners):
        build_patches(tab, field, into(pc, j), 3, c, ends[COLUMNS[c][0]], ends[COLUMNS[c][1]])

    flip(w2, w2f)

    def hide(pre):
        return rounded(pre * jax.nn.sigmoid(pre))

    def own_pairs(patch, i):
        results = pairs([lambda j, b, g=g: patch[4 * i + g + j, b : b + BE] for g in (0, 2)], wide)
        return [(4 * i + 2 * g + h, results[g][h].reshape(BE, ROWS, C)) for g in range(2) for h in range(2)]

    def y_pairs(m):
        gets = [lambda j, b, s=s, p=p: py[s, 2 * p + j, b : b + m] for s in range(2) for p in range(4)]
        results = pairs(gets, wide)
        return [
            (s, 2 * p + h, results[4 * s + p][h].reshape(m, ROWS, C)) for s in range(2) for p in range(4) for h in range(2)
        ]

    def first_own(i, unused):
        for at, pre in own_pairs(p1, i):
            slope1[at] = slope_of(pre)
            hid[2 + at, 2:10, 0:ROWS, :] = hide(pre)
        return unused

    for i in range(2):
        first_own(i, 0)
    results = pairs([lambda j, b, s=s: px[s, j, b : b + BE] for s in range(2)], wide)
    for s in range(2):
        for h in range(2):
            hid[10 * s + h, 2:10, 0:ROWS, :] = hide(results[s][h]).reshape(BE, ROWS, C)
    for s, at, pre in y_pairs(2):
        hid[2 + at, 10 * s : 10 * s + 2, 0:ROWS, :] = hide(pre)
    [result] = pairs([lambda j, b: pc[:, j, b : b + 2]], wide)
    for h in range(2):
        value = hide(result[h]).reshape(4, 2, ROWS, C)
        for j, (ax, ay) in enumerate(((0, 0), (0, 10), (10, 0), (10, 10))):
            hid[ax + h, ay : ay + 2, 0:ROWS, :] = value[j]

    ends = spans(1)
    band(w2, wide)
    build_patches(tab, hid, into(p2), 2, OWN, ends[0], ends[0])
    for j, cx in enumerate((-1, 1)):
        build_patches(tab, hid, into(px, j), 2, COLUMNS.index((cx, 0)), ends[cx], ends[0])
        build_patches(tab, hid, into(py, j), 2, COLUMNS.index((0, cx)), ends[0], ends[cx])
    for j, c in enumerate(corners):
        build_patches(tab, hid, into(pc, j), 2, c, ends[COLUMNS[c][0]], ends[COLUMNS[c][1]])

    def second_own(i, unused):
        for at, pre in own_pairs(p2, i):
            total = field[3 + at, 3:11, 0:ROWS, :] * live + pre
            sig = jax.nn.sigmoid(total)
            out[at] = (total * sig * live).astype(BF16)
            slope = sig * (1.0 + total * (1.0 - sig))
            grad = (cot[at].astype(F32) * slope * live).astype(BF16)
            b2o[at] = grad
            back[1 + at, 1:9, 0:ROWS, :] = grad.astype(F32)
        return unused

    for i in range(2):
        second_own(i, 0)
    for s, at, pre in y_pairs(1):
        near = (ym, yp)[s]
        total = field[3 + at, (2, 11)[s], 0:ROWS, :] + pre[0]
        back[1 + at, 9 * s, 0:ROWS, :] = rounded(near[24 + at].astype(F32) * slope_of(total))
    pre = product(lambda a, b: px[:, a : a + 1, b : b + BE], w2).reshape(2, BE, ROWS, C)
    for j, (at, cx, near) in enumerate(((2, 0, xm), (11, 9, xp))):
        total = field[at, 3:11, 0:ROWS, :] + pre[j]
        back[cx, 1:9, 0:ROWS, :] = rounded(near[24:32].astype(F32) * slope_of(total))
    pre = product(lambda a, b: pc[:, a : a + 1, b : b + 1], w2).reshape(4, ROWS, C)
    for j, (ax, ay, cx, cy, near, at) in enumerate(
        ((2, 2, 0, 0, qm, 18), (2, 11, 0, 9, qp, 18), (11, 2, 9, 0, qm, 19), (11, 11, 9, 9, qp, 19))
    ):
        total = field[ax, ay, 0:ROWS, :] + pre[j]
        back[cx, cy, 0:ROWS, :] = rounded(near[at].astype(F32) * slope_of(total))
    @pl.when(core[0] >= 0)
    def second_weight_grad():
        weight_grad(p2, b2o, turned, gr, 1 - core[0], scale)

    band(w2f, wide)
    build_patches(tab, back, into(p2), 1, OWN, (0, BE), (0, BE))

    def third(i, unused):
        for at, pre in own_pairs(p2, i):
            b1o[at] = (pre * slope1[at] * live).astype(BF16)
        return unused

    for i in range(2):
        third(i, 0)
    elow[...] = b1o[0]
    ehigh[...] = b1o[7]
    @pl.when(core[0] >= 0)
    def first_weight_grad():
        weight_grad(p1, b1o, turned, gr, core[0], scale)


def last_kernel(own, b1, b2, xm, xp, ym, yp, w1, out, field, patch, w1f, wide, staged, tab, sem):
    load_tables({OWN: (own, 0)}, staged, tab, sem)
    live = live_rows(tab)
    zero_slot(field)
    clear_band(wide)
    flip(w1, w1f)
    band(w1f, wide)

    def fill(i, unused):
        field[1 + i, 1:9, 0:ROWS, :] = b1[i].astype(F32)
        return unused

    lax.fori_loop(0, BE, fill, 0)
    field[0, 1:9, 0:ROWS, :] = xm[...].astype(F32)
    field[9, 1:9, 0:ROWS, :] = xp[...].astype(F32)
    field[:, 0, 0:ROWS, :] = ym[...].astype(F32)
    field[:, 9, 0:ROWS, :] = yp[...].astype(F32)
    build_patches(tab, field, into(patch), 1, OWN, (0, BE), (0, BE))

    def step(i, unused):
        results = pairs([lambda j, b, g=g: patch[4 * i + g + j, b : b + BE] for g in (0, 2)], wide)
        for g in range(2):
            for h in range(2):
                at = 4 * i + 2 * g + h
                out[at] = ((b2[at].astype(F32) + results[g][h].reshape(BE, ROWS, C)) * live).astype(BF16)
        return unused

    for i in range(2):
        step(i, 0)


def call(kernel, outs, scratch, cost, mib, scalars, far, *args):
    smem = pl.BlockSpec(memory_space=pltpu.SMEM)
    vmem = pl.BlockSpec(memory_space=pltpu.VMEM)
    anywhere = pl.BlockSpec(memory_space=pltpu.HBM)
    args = [
        pltpu.with_memory_space_constraint(arg, pltpu.HBM) if scalars <= i < scalars + far else arg
        for i, arg in enumerate(args)
    ]
    return pl.pallas_call(
        kernel,
        out_shape=outs,
        in_specs=[smem] * scalars + [anywhere] * far + [vmem] * (len(args) - scalars - far),
        out_specs=jax.tree.map(lambda o: vmem, outs),
        scratch_shapes=scratch,
        compiler_params=pltpu.CompilerParams(vmem_limit_bytes=mib * 2**20),
        cost_estimate=pl.CostEstimate(flops=cost[0], bytes_accessed=cost[1], transcendentals=0),
    )(*args)


def swap_cores(part):
    return lax.ppermute(part, "dp", [(0, 1), (1, 0)])


def sum_scatter(part, axis):
    n = lax.axis_size(axis)
    swapped = lax.all_to_all(part.reshape(n, part.shape[0] // n, C), axis, 0, 0, tiled=True)
    return jnp.sum(swapped.astype(F32), axis=0).astype(BF16)


def sum_pairs(part, axis):
    n = lax.axis_size(axis)
    reach = 1
    while reach < n:
        other = lax.ppermute(part, axis, [(i, i ^ (2 * reach - 1)) for i in range(n)])
        part = (part.astype(F32) + other.astype(F32)).astype(BF16)
        reach *= 2
    return part


def gather_axis(part, axis):
    n = lax.axis_size(axis)
    copies = jnp.broadcast_to(part[None], (n,) + part.shape)
    return lax.all_to_all(copies, axis, 0, 0, tiled=True).reshape(n * part.shape[0], C)


def shape_of(*sizes):
    return jax.ShapeDtypeStruct(sizes, BF16)


def shards(features, cotangent, first_weight, second_weight, neighbours, counts):
    x = features.reshape(BE, BE, ROWS, C)
    cot = cotangent.reshape(BE, BE, ROWS, C)
    w1, w2 = first_weight.reshape(27 * C, C), second_weight.reshape(27 * C, C)
    n_devices = lax.axis_size("sx") * lax.axis_size("sy") * lax.axis_size("dp")
    scale = float(n_devices * NB * BE**3) ** -0.5
    core = lax.axis_index("dp").astype(jnp.int32)

    payload = shape_of(33, ROWS, C)
    xlow, xhigh, ylow, yhigh, own = call(
        first_payload_kernel, [payload] * 4 + [shape_of(1, ROWS, C)],
        [pltpu.VMEM((BE, BE, ROWS, C), BF16)] * 2 + [pltpu.SemaphoreType.DMA((2,))], (0, 2**21), 8, 2, 2,
        neighbours.reshape(NB, 26), counts.reshape(1), x, cot,
    )
    xm, xp = shift_pair(xlow, xhigh, "sx")
    ym, yp = shift_pair(ylow, yhigh, "sy")
    qlow, qhigh = call(corner_payload_kernel, [shape_of(22, ROWS, C)] * 2, [], (0, 2**19), 8, 0, 0, xm, xp)
    qm, qp = shift_pair(qlow, qhigh, "sy")

    block, edge = shape_of(BE, BE, ROWS, C), shape_of(BE, ROWS, C)
    lanes = 3 * C
    unit = 2 * BE * BE * ROWS * 27 * C * C
    tables = [pltpu.VMEM((16, C), jnp.int32), pltpu.SMEM((16, C), jnp.int32), pltpu.SemaphoreType.DMA]
    out, b2, b1, elow, ehigh, grads = call(
        functools.partial(main_kernel, scale),
        [block, block, block, edge, edge, shape_of(2, 27 * C, C)],
        [
            *[pltpu.VMEM((BE, BE, ROWS, C), BF16)] * 2,
            *[pltpu.VMEM((27 * C, C), BF16)] * 3,
            pltpu.SemaphoreType.DMA((4,)),
            pltpu.VMEM((14, 14, ROWS + BE, C), F32),
            pltpu.VMEM((12, 12, ROWS + BE, C), F32),
            pltpu.VMEM((10, 10, ROWS + BE, C), F32),
            pltpu.VMEM((10, 10, ROWS, lanes), BF16),
            pltpu.VMEM((10, 10, ROWS, lanes), BF16),
            pltpu.VMEM((2, 4, 10, ROWS, lanes), BF16),
            pltpu.VMEM((2, 10, 4, ROWS, lanes), BF16),
            pltpu.VMEM((4, 4, 4, ROWS, lanes), BF16),
            pltpu.VMEM((BE, BE, ROWS, C), F32),
            pltpu.VMEM((3 * C, (BE + 2) * BE * ROWS), BF16),
            pltpu.VMEM((36 * C, 2 * C), BF16),
            *tables,
        ],
        (7 * unit, 10 * 2**20), 36, 1, 4,
        core.reshape(1), x, cot, w1, w2, xm, xp, ym, yp, qm, qp, own,
    )

    received = swap_cores(grads[1])
    bxm, bxp = shift_pair(elow, ehigh, "sx")
    part = (grads[0].astype(F32) + received.astype(F32)).astype(BF16)
    part, bxm, bxp = lax.optimization_barrier((sum_scatter(part, "sy"), bxm, bxp))
    blow, bhigh = call(edge_payload_kernel, [shape_of(BE + 2, ROWS, C)] * 2, [], (0, 2**19), 8, 0, 0, bxm, bxp, b1)
    bym, byp = shift_pair(blow, bhigh, "sy")
    part, bym, byp, b2 = lax.optimization_barrier((sum_pairs(part, "sx"), bym, byp, b2))

    grad_input = call(
        last_kernel,
        block,
        [
            pltpu.VMEM((10, 10, ROWS + BE, C), F32),
            pltpu.VMEM((10, 10, ROWS, lanes), BF16),
            pltpu.VMEM((27 * C, C), BF16),
            pltpu.VMEM((36 * C, 2 * C), BF16),
            *tables,
        ],
        (unit, 4 * 2**20), 12, 0, 0,
        own, b1, b2, bxm, bxp, bym, byp, w1,
    )
    part, grad_input = lax.optimization_barrier((gather_axis(part, "sy"), grad_input))
    part = part.reshape(27, C, C)
    other = swap_cores(part)
    first = jnp.where(core == 0, part, other).astype(F32)
    second = jnp.where(core == 0, other, part).astype(F32)
    shape = features.shape
    return out.reshape(shape), grad_input.reshape(shape), first, second


def solution(mesh):
    column = P("dp", "sx", "sy", None, None, None)
    return jax.shard_map(
        shards,
        mesh=mesh,
        in_specs=(column, column, P(), P(), P("dp", "sx", "sy", None, None), P("dp", "sx", "sy")),
        out_specs=(column, column, P(), P()),
        check_vma=False,
    )
```
